32 devices in a mesh: leaf: 16 (over z, y, x), panel: 2 (over core).
Axes of the slice: x: 2, y: 2, z: 4, core: 2. Of those that a mesh axis runs over, the one named last changes fastest.
Arguments:
- rhs: float32 [32768, 128], P(('leaf', 'panel')), may hold values from -6 to 6
- leaf_q: float32 [64, 512, 512], P(('leaf', 'panel')), may hold values from -0.25 to 0.25
- leaf_e: float32 [64, 384, 384], P(('leaf', 'panel')), may hold values from -0.3125 to 0.3125
- leaf_f: float32 [64, 128, 384], P(('leaf', 'panel')), may hold values from -0.15625 to 0.15625
- leaf_g: float32 [64, 384, 128], P(('leaf', 'panel')), may hold values from -0.25 to 0.25
- mid_q: float32 [32, 256, 256], P(('leaf', 'panel')), may hold values from -0.375 to 0.375
- mid_e: float32 [32, 128, 128], P(('leaf', 'panel')), may hold values from -0.5 to 0.5
- mid_f: float32 [32, 128, 128], P(('leaf', 'panel')), may hold values from -0.25 to 0.25
- mid_g: float32 [32, 128, 128], P(('leaf', 'panel')), may hold values from -0.25 to 0.25
- pair_q: float32 [16, 256, 256], P('leaf'), may hold values from -0.375 to 0.375
- pair_e: float32 [16, 128, 128], P('leaf'), may hold values from -0.5 to 0.5
- pair_f: float32 [16, 128, 128], P('leaf'), may hold values from -0.25 to 0.25
- pair_g: float32 [16, 128, 128], P('leaf'), may hold values from -0.25 to 0.25
- up_q: float32 [16, 256, 256], P('leaf'), may hold values from -0.375 to 0.375
- up_e: float32 [16, 128, 128], P('leaf'), may hold values from -0.5 to 0.5
- up_f: float32 [16, 128, 128], P('leaf'), may hold values from -0.25 to 0.25
- up_g: float32 [16, 128, 128], P('leaf'), may hold values from -0.25 to 0.25
Outputs:
- solution: float32 [32768, 128], P(('leaf', 'panel'))
The draws below stay inside these ranges and needn't reach their ends.
All inputs are finite; a program needn't handle non-finite values.
Results may differ from the reference program's by a relative error of at most 0.0003.
Values sent between devices are 32-bit elements; how exact they have to be, the bound alone decides.
No kernel may reach another device: no remote copies, remote signals or barrier semaphores. Data moves between devices by JAX's collectives and lax.ppermute only.
A program may use at most 128 MiB of HBM per device.

```python
import jax
import jax.numpy as jnp
import numpy as np
from jax import lax

LEAF = 512
RANK = 128
COLS = 128
LEAVES_DEV = 2
LEAVES = 64
MID = 32
TREE_DEPTH = 4
LOCAL_DEPTH = 1
N_LEAF = 16
N_PANEL = 2


def shard_levels(key, dims, pieces, smallest, high):
    factor_of = 1.0
    for dim, parts in pieces:
        draws = jax.random.uniform(jax.random.fold_in(jax.random.fold_in(key, 6), dim), (parts,), jnp.float32, smallest / len(pieces), high / len(pieces))
        factor_of = factor_of * jnp.repeat(jnp.exp(draws), dims[dim] // parts).reshape((-1,) + (1,) * (len(dims) - 1 - dim))
    return factor_of


def noise(rng, dims, scale, bound, cuts=(), kind=jnp.bfloat16):
    values = scale * jax.random.normal(rng, dims, jnp.float32)
    if cuts:
        values = values * shard_levels(rng, dims, cuts, -0.22, 0.18)
    return jnp.clip(values, -bound, bound).astype(kind)


def setup_inputs(seed: int = 0) -> dict:
    key_list = jax.random.split(jax.random.key(seed), 18)
    rhs = noise(key_list[0], (LEAVES * LEAF, COLS), 1.0, 6.0, ((0, 32),), jnp.float32)
    leaf_q = noise(key_list[1], (LEAVES, LEAF, LEAF), LEAF ** -0.5, 0.25, ((0, 32),), jnp.float32)
    leaf_e = noise(key_list[2], (LEAVES, LEAF - RANK, LEAF - RANK), (LEAF - RANK) ** -0.5, 0.3125, ((0, 32),), jnp.float32)
    leaf_f = noise(key_list[3], (LEAVES, RANK, LEAF - RANK), (4 * (LEAF - RANK)) ** -0.5, 0.15625, ((0, 32),), jnp.float32)
    leaf_g = noise(key_list[4], (LEAVES, LEAF - RANK, RANK), (4 * RANK) ** -0.5, 0.25, ((0, 32),), jnp.float32)
    mid_q = noise(key_list[5], (MID, 2 * RANK, 2 * RANK), (2 * RANK) ** -0.5, 0.375, ((0, 32),), jnp.float32)
    mid_e = noise(key_list[6], (MID, RANK, RANK), RANK ** -0.5, 0.5, ((0, 32),), jnp.float32)
    mid_f = noise(key_list[7], (MID, RANK, RANK), (4 * RANK) ** -0.5, 0.25, ((0, 32),), jnp.float32)
    mid_g = noise(key_list[8], (MID, RANK, RANK), (4 * RANK) ** -0.5, 0.25, ((0, 32),), jnp.float32)
    pair_q = noise(key_list[9], (N_LEAF, 2 * RANK, 2 * RANK), (2 * RANK) ** -0.5, 0.375, ((0, 16),), jnp.float32)
    pair_e = noise(key_list[10], (N_LEAF, RANK, RANK), RANK ** -0.5, 0.5, ((0, 16),), jnp.float32)
    pair_f = noise(key_list[11], (N_LEAF, RANK, RANK), (4 * RANK) ** -0.5, 0.25, ((0, 16),), jnp.float32)
    pair_g = noise(key_list[12], (N_LEAF, RANK, RANK), (4 * RANK) ** -0.5, 0.25, ((0, 16),), jnp.float32)
    up_q = noise(key_list[13], (N_LEAF, 2 * RANK, 2 * RANK), (2 * RANK) ** -0.5, 0.375, ((0, 16),), jnp.float32)
    up_e = noise(key_list[14], (N_LEAF, RANK, RANK), RANK ** -0.5, 0.5, ((0, 16),), jnp.float32)
    up_f = noise(key_list[15], (N_LEAF, RANK, RANK), (4 * RANK) ** -0.5, 0.25, ((0, 16),), jnp.float32)
    up_g = noise(key_list[16], (N_LEAF, RANK, RANK), (4 * RANK) ** -0.5, 0.25, ((0, 16),), jnp.float32)
    return {"rhs": rhs, "leaf_q": leaf_q, "leaf_e": leaf_e, "leaf_f": leaf_f, "leaf_g": leaf_g, "mid_q": mid_q, "mid_e": mid_e, "mid_f": mid_f, "mid_g": mid_g, "pair_q": pair_q, "pair_e": pair_e, "pair_f": pair_f, "pair_g": pair_g, "up_q": up_q, "up_e": up_e, "up_f": up_f, "up_g": up_g}


highest_precision = lax.Precision.HIGHEST


def eliminate(basis, inverse_factor, coupling_block, block_in):
    eliminated_rows = inverse_factor.shape[1]
    coefficient_rows = jnp.einsum('nij,nic->njc', basis, block_in, precision=highest_precision)
    lower_block_part = jnp.einsum('gwe,gel->gwl', inverse_factor, coefficient_rows[:, :eliminated_rows], precision=highest_precision)
    reduced_system = coefficient_rows[:, eliminated_rows:] - jnp.einsum('gwe,gel->gwl', coupling_block, lower_block_part, precision=highest_precision)
    return lower_block_part, reduced_system


def substitute(basis, back_map, lower_block_part, upper_part):
    first_part = lower_block_part - jnp.einsum('gwe,gel->gwl', back_map, upper_part, precision=highest_precision)
    stacked = jnp.concatenate([first_part, upper_part], axis=1)
    return jnp.einsum('nij,njc->nic', basis, stacked, precision=highest_precision)


def reference(rhs, leaf_q, leaf_e, leaf_f, leaf_g, mid_q, mid_e, mid_f, mid_g, pair_q, pair_e, pair_f, pair_g, up_q, up_e, up_f, up_g):
    blocks = N_LEAF * N_PANEL
    columns = rhs.shape[1]
    leaf_count = rhs.shape[0] // LEAF
    leaf_lower, reduced_system = eliminate(leaf_q, leaf_e, leaf_f, rhs.reshape(leaf_count, LEAF, columns))

    def mid_slice(table, offset, pairs):
        shaped = table.reshape((blocks, LEAVES_DEV - 1) + table.shape[1:])
        return shaped[:, offset:offset + pairs].reshape((blocks * pairs,) + table.shape[1:])

    mid_saved = []
    nodes_now = LEAVES_DEV
    offset = 0
    for section_idx in range(LOCAL_DEPTH):
        pairs = nodes_now // 2
        stacked = reduced_system.reshape(blocks * pairs, 2 * RANK, columns)
        lower_block_part, reduced_system = eliminate(mid_slice(mid_q, offset, pairs), mid_slice(mid_e, offset, pairs), mid_slice(mid_f, offset, pairs), stacked)
        mid_saved.append((lower_block_part, offset, pairs))
        offset = offset + pairs
        nodes_now = pairs
    pair_lower, reduced_system = eliminate(pair_q, pair_e, pair_f, reduced_system.reshape(N_LEAF, 2 * RANK, columns))
    upper_saved = []
    for level in range(1, TREE_DEPTH + 1):
        nodes_now = N_LEAF >> level
        slots = (2 * np.arange(nodes_now) + 1) * (1 << (level - 1))
        stacked = reduced_system.reshape(nodes_now, 2 * RANK, columns)
        lower_block_part, reduced_system = eliminate(up_q[slots], up_e[slots], up_f[slots], stacked)
        upper_saved.append((lower_block_part, slots))
    upper_part = jnp.einsum('gwe,gel->gwl', up_e[0:1], reduced_system, precision=highest_precision)
    for level in range(TREE_DEPTH, 0, -1):
        lower_block_part, slots = upper_saved[level - 1]
        whole_x = substitute(up_q[slots], up_g[slots], lower_block_part, upper_part)
        upper_part = whole_x.reshape(2 * whole_x.shape[0], RANK, columns)
    whole_x = substitute(pair_q, pair_g, pair_lower, upper_part)
    upper_part = whole_x.reshape(blocks, RANK, columns)
    for lower_block_part, offset, pairs in reversed(mid_saved):
        whole_x = substitute(mid_slice(mid_q, offset, pairs), mid_slice(mid_g, offset, pairs), lower_block_part, upper_part)
        upper_part = whole_x.reshape(2 * whole_x.shape[0], RANK, columns)
    result = substitute(leaf_q, leaf_g, leaf_lower, upper_part)
    return result.reshape(leaf_count * LEAF, columns)
```

```python
import functools

import jax
import jax.numpy as jnp
from jax import lax
from jax.experimental import pallas as pl
from jax.experimental.pallas import tpu as pltpu
from jax.sharding import PartitionSpec as P

F32 = jnp.float32
VMEM = pl.BlockSpec(memory_space=pltpu.VMEM)
ANY = pl.BlockSpec(memory_space=pl.ANY)
NN = (((1,), (0,)), ((), ()))
NT = (((1,), (1,)), ((), ()))


def split(value):
    high = value.astype(jnp.bfloat16)
    return high, (value - high.astype(F32)).astype(jnp.bfloat16)


def product(left, right, dims):
    left_high, left_low = left if isinstance(left, tuple) else split(left)
    right_high, right_low = right if isinstance(right, tuple) else split(right)
    dot = functools.partial(lax.dot_general, dimension_numbers=dims, preferred_element_type=F32)
    return dot(left_high, right_high) + (dot(left_high, right_low) + dot(left_low, right_high))


def mm(left, right):
    return product(left, right, NN)


def mt(left, right):
    return product(left, right, NT)


def call(kernel, out_shapes, *operands, any_inputs=False, scratch=(), flops=0):
    outs = [jax.ShapeDtypeStruct(shape, F32) for shape in out_shapes]
    size = sum(4 * o.size for o in operands) + sum(4 * o.size for o in outs)
    return pl.pallas_call(
        kernel,
        out_shape=outs,
        in_specs=[ANY if any_inputs else VMEM] * len(operands),
        out_specs=[VMEM] * len(outs),
        scratch_shapes=list(scratch),
        compiler_params=pltpu.CompilerParams(vmem_limit_bytes=40 * 2**20),
        cost_estimate=pl.CostEstimate(flops=flops, bytes_accessed=size, transcendentals=0),
    )(*operands)


def fetch(sources, targets, sems):
    copies = [
        pltpu.make_async_copy(s, t, sems.at[i]) for i, (s, t) in enumerate(zip(sources, targets))
    ]
    for copy in copies:
        copy.start()
    return copies


def up_rows(basis, inverse_factor, coupling_block, block_rows):
    e = inverse_factor.shape[0]
    c = mm(block_rows, basis)
    y = mt(c[:, :e], inverse_factor)
    return y, c[:, e:] - mt(y, coupling_block)


def node_kernel(q_ref, e_ref, f_ref, g_ref, low_ref, high_ref):
    rank = e_ref.shape[1]
    q = q_ref[0]
    q1, q2 = split(q[:, :rank]), q[:, rank:]
    inverse = split(e_ref[0])
    fe = mm(f_ref[0], inverse)
    s = q2.T - mt(fe, q1)
    v = mm(q1, inverse)
    a = mt(v, q1)
    t = q2 - mm(q1, g_ref[0])
    for half, ref in enumerate((low_ref, high_ref)):
        rows = slice(half * rank, (half + 1) * rank)
        ref[0] = s[:, :rank]
        ref[1] = s[:, rank:]
        ref[2] = a[rows, :rank]
        ref[3] = a[rows, rank:]
        ref[4] = t[rows]
    first = lax.axis_index("leaf") == 0

    @pl.when(first)
    def _():
        low_ref[4] = e_ref[0]


def top_kernel(low_ref, high_ref, apex_ref, out_low_ref, out_high_ref):
    apex = split(apex_ref[4])
    s = [split(low_ref[0]), split(low_ref[1])]
    for ref, out in ((low_ref, out_low_ref), (high_ref, out_high_ref)):
        u = split(mm(ref[4], apex))
        out[0] = ref[2] + mm(u, s[0])
        out[1] = ref[3] + mm(u, s[1])


def leaf_kernel(
    rhs, q, e, f, mid_q, mid_e, mid_f, y_ref, mid_y_ref, z_ref,
    rhs_v, q_v, e_v, f_v, mid_q_v, mid_e_v, mid_f_v, sems,
):
    leaves = q.shape[0]
    size = q.shape[1]
    sources, targets = [], []
    for n in range(leaves):
        rows = pl.ds(n * size, size)
        sources += [rhs.at[rows], q.at[n], e.at[n], f.at[n]]
        targets += [rhs_v.at[rows], q_v.at[n], e_v.at[n], f_v.at[n]]
    sources += [mid_q, mid_e, mid_f]
    targets += [mid_q_v, mid_e_v, mid_f_v]
    copies = fetch(sources, targets, sems)
    reduced = []
    for n in range(leaves):
        copies[4 * n].wait()
        copies[4 * n + 1].wait()
        block = rhs_v[n * size : (n + 1) * size, :].T
        c = mm(block, q_v[n])
        copies[4 * n + 2].wait()
        count = e.shape[1]
        y = mt(c[:, :count], e_v[n])
        copies[4 * n + 3].wait()
        reduced.append(c[:, count:] - mt(y, f_v[n]))
        y_ref[n] = y
    for copy in copies[4 * leaves :]:
        copy.wait()
    y, z = up_rows(mid_q_v[0], mid_e_v[0], mid_f_v[0], jnp.concatenate(reduced, axis=1))
    mid_y_ref[...] = y
    z_ref[...] = z


def pair_kernel(own_ref, other_ref, q_ref, e_ref, f_ref, y_ref, z_ref):
    second = lax.axis_index("panel") == 1
    own, other = own_ref[...], other_ref[...]
    block = jnp.concatenate(
        [jnp.where(second, other, own), jnp.where(second, own, other)], axis=1
    )
    y, z = up_rows(q_ref[0], e_ref[0], f_ref[0], block)
    y_ref[...] = y
    z_ref[...] = z


def level_kernel(bit, own_ref, other_ref, packet_ref, z_ref):
    second = (lax.axis_index("leaf") >> bit) & 1 == 1
    own, other = own_ref[...], other_ref[...]
    first_z = jnp.where(second, other, own)
    second_z = jnp.where(second, own, other)
    z_ref[...] = mt(first_z, packet_ref[0]) + mt(second_z, packet_ref[1])


def own_half(ref, start, rank):
    return ref[0, pl.ds(pl.multiple_of(start * rank, rank), rank), :]


def tail_kernel(
    q, g, y_ref, mid_q_ref, mid_g_ref, mid_y_ref, pair_q_ref, pair_g_ref, pair_y_ref,
    base_ref, w_ref, q_v, g_v, sems,
):
    leaves, size = q.shape[0], q.shape[1]
    rank = pair_g_ref.shape[2]
    count = g.shape[1]
    copies = fetch(
        [a.at[n] for n in range(leaves) for a in (q, g)],
        [a.at[n] for n in range(leaves) for a in (q_v, g_v)],
        sems,
    )
    pair_q = own_half(pair_q_ref, lax.axis_index("panel"), rank)
    pair_t = split(pair_q[:, rank:] - mm(pair_q[:, :rank], pair_g_ref[0]))
    mid_w = mt(pair_y_ref[...], pair_q[:, :rank])
    mid_q = mid_q_ref[0]
    mid_q1 = split(mid_q[:, :rank])
    mid_t = split(mid_q[:, rank:] - mm(mid_q1, mid_g_ref[0]))
    leaf_w = mt(mid_y_ref[...], mid_q1) + mt(mid_w, mid_t)
    map_w = mm(mid_t, pair_t)
    for n in range(leaves):
        copies[2 * n].wait()
        q1 = split(q_v[n, :, :count])
        copies[2 * n + 1].wait()
        leaf_t = split(q_v[n, :, count:] - mm(q1, g_v[n]))
        part = slice(n * rank, (n + 1) * rank)
        rows = slice(n * size, (n + 1) * size)
        base_ref[rows] = mt(q1, y_ref[n]) + mt(leaf_t, leaf_w[:, part])
        w_ref[rows] = mm(leaf_t, map_w[part])


def fold_kernel(levels, base_ref, w_ref, *refs):
    base_out, w_out = refs[-2:]
    offset = None
    chain = None
    for bit in range(levels):
        own_ref, other_ref, packet_ref = refs[3 * bit : 3 * bit + 3]
        second = (lax.axis_index("leaf") >> bit) & 1 == 1
        own, other = own_ref[...], other_ref[...]
        first_z = jnp.where(second, other, own)
        second_z = jnp.where(second, own, other)
        u = mt(first_z, packet_ref[2]) + mt(second_z, packet_ref[3])
        if bit == 0:
            offset, chain = u, packet_ref[4]
        else:
            chain = split(chain)
            offset = offset + mt(u, chain)
            chain = mm(chain, packet_ref[4])
    w = split(w_ref[...])
    base_out[...] = base_ref[...] + mt(w, offset)
    w_out[...] = mm(w, chain)


def apex_kernel(low, levels, *refs):
    out_ref = refs[-1]
    w = None
    for bit in range(levels - 1, low - 1, -1):
        own_ref, other_ref, packet_ref = refs[3 * (bit - low) : 3 * (bit - low) + 3]
        second = (lax.axis_index("leaf") >> bit) & 1 == 1
        own, other = own_ref[...], other_ref[...]
        first_z = jnp.where(second, other, own)
        second_z = jnp.where(second, own, other)
        start = 0 if bit == levels - 1 else 2
        value = mt(first_z, packet_ref[start]) + mt(second_z, packet_ref[start + 1])
        if w is not None:
            value = value + mt(w, packet_ref[4])
        w = value
    out_ref[...] = w


def last_kernel(base_ref, w_ref, incoming_ref, out_ref):
    out_ref[...] = base_ref[...] + mt(w_ref[...], incoming_ref[...])


HOME = (0, 1, 1, 0)


def home_core(level):
    return HOME[(level - 1) % 4]


def packet_rounds(depth, low):
    rounds = []
    holders = {k: {(2 * j + 1) << (k - 1) for j in range(1 << (depth - k))} for k in range(1, depth + 1)}
    for r in range(1, depth + 2):
        moves = []
        for level in range(1, depth + 1):
            if level == depth and r == 1:
                moves.append((level, -1, [(0, 1 << (depth - 1))]))
                continue
            bit = level - r + (1 if level == depth else 0)
            if bit < (0 if level <= low else low):
                continue
            pairs = [(p, p ^ (1 << bit)) for p in sorted(holders[level])]
            holders[level] |= {target for _, target in pairs}
            moves.append((level, bit, pairs))
        if moves:
            rounds.append(moves)
    return rounds


def local(
    rhs, leaf_q, leaf_e, leaf_f, leaf_g, mid_q, mid_e, mid_f, mid_g,
    pair_q, pair_e, pair_f, pair_g, up_q, up_e, up_f, up_g,
):
    count_leaf = lax.axis_size("leaf")
    cores = lax.axis_size("panel")
    depth = count_leaf.bit_length() - 1
    low = min(2, depth - 1)
    position = lax.axis_index("leaf")
    core = lax.axis_index("panel")
    rank, columns = up_e.shape[1], rhs.shape[1]
    leaves, size = leaf_q.shape[0], leaf_q.shape[1]
    count = leaf_e.shape[1]
    tile = (columns, rank)
    dma = pltpu.SemaphoreType.DMA

    def swap_cores(value):
        return lax.ppermute(value, "panel", [(i, cores - 1 - i) for i in range(cores)])

    def exchange(value, bit, step):
        pairs = [(p, p ^ (1 << bit)) for p in range(0, count_leaf, step)]
        return lax.ppermute(value, "leaf", pairs)

    packet = (5, rank, rank)
    low_half, high_half = call(node_kernel, [packet, packet], up_q, up_e, up_f, up_g)
    held = {}

    rounds = packet_rounds(depth, low)
    full = {}

    def bit_at(level, bit):
        return position & ((1 << level) - 1) == (1 << bit)

    def start_round(index):
        moves = rounds[index]
        received = {}
        groups = {0: [m for m in moves if home_core(m[0]) == 0], 1: [m for m in moves if home_core(m[0]) == 1]}
        for i in range(max(len(groups[0]), len(groups[1]))):
            ops = [groups[c][i] for c in (0, 1) if i < len(groups[c])]
            pairs = []
            for level, _, list_of in ops:
                c = home_core(level)
                pairs += [(p * cores + c, t * cores + c) for p, t in list_of]
            if index == 0:
                operand = low_half
            else:
                values = [held[level] if bit != depth - 1 else top_low for level, bit, _ in ops]
                if len(values) == 2:
                    a, b = values
                    n = max(a.shape[0], b.shape[0])
                    a = jnp.pad(a, ((0, n - a.shape[0]), (0, 0), (0, 0)))
                    b = jnp.pad(b, ((0, n - b.shape[0]), (0, 0), (0, 0)))
                    operand = jnp.where(core == home_core(ops[0][0]), a, b)
                else:
                    operand = values[0]
            incoming = lax.ppermute(operand, ("leaf", "panel"), pairs)
            for level, _, _ in ops:
                received[level] = incoming
        return received

    def finish_round(index, received):
        nonlocal top_low
        moves = rounds[index]
        finished = []
        for level, bit, _ in moves:
            value = received[level]
            if level == depth:
                if bit < 0:
                    top_low, held[level] = call(
                        top_kernel, [(2, rank, rank)] * 2, low_half, high_half, value
                    )
                else:
                    held[level] = jnp.where(bit_at(bit + 1, bit), held[level], value[:2]) if bit == depth - 1 else jnp.where(bit_at(bit + 1, bit), value[:2], held[level])
            elif index == 0:
                owner = bit_at(level, level - 1)
                held[level] = jnp.where(owner, high_half, value)
            else:
                held[level] = jnp.where(bit_at(bit + 1, bit), value, held[level])
            if bit == (0 if level <= low else low):
                finished.append(level)
        for c0 in range(0, len(finished), 1):
            level = finished[c0]
            if level in full:
                continue
            mate = next((o for o in finished if o not in full and home_core(o) != home_core(level) and held[o].shape == held[level].shape), None)
            mine = core == home_core(level)
            if mate is None:
                other = swap_cores(held[level])
                full[level] = jnp.where(mine, held[level], other)
            else:
                other = swap_cores(jnp.where(mine, held[level], held[mate]))
                full[level] = jnp.where(mine, held[level], other)
                full[mate] = jnp.where(mine, other, held[mate])

    top_low = None
    flying = start_round(0)

    y, mid_y, z = call(
        leaf_kernel,
        [(leaves, columns, count), tile, tile],
        rhs, leaf_q, leaf_e, leaf_f, mid_q, mid_e, mid_f,
        any_inputs=True,
        scratch=[
            pltpu.VMEM(a.shape, F32) for a in (rhs, leaf_q, leaf_e, leaf_f, mid_q, mid_e, mid_f)
        ] + [dma((4 * leaves + 3,))],
    )
    other = swap_cores(z)
    pair_y, z = call(pair_kernel, [tile, tile], z, other, pair_q, pair_e, pair_f)

    exchanged = []
    base = weight = None
    for bit in range(depth):
        other = exchange(z, bit, 1 if bit < low else 1 << low)
        exchanged += [z, other]
        if bit < len(rounds):
            finish_round(bit, flying)
            if bit + 1 < len(rounds):
                flying = start_round(bit + 1)
        if bit == 0:
            base, weight = call_tail(
                leaf_q, leaf_g, y, mid_q, mid_g, mid_y, pair_q, pair_g, pair_y, rhs.shape
            )
        if bit < depth - 1:
            (z,) = call(functools.partial(level_kernel, bit), [tile], z, other, full[bit + 1])
    for index in range(depth, len(rounds)):
        finish_round(index, flying)
        if index + 1 < len(rounds):
            flying = start_round(index + 1)

    folded = []
    for bit in range(low):
        folded += [exchanged[2 * bit], exchanged[2 * bit + 1], full[bit + 1]]
    base, weight = call(
        functools.partial(fold_kernel, low), [base.shape, weight.shape], base, weight, *folded
    )

    above = []
    for bit in range(low, depth):
        above += [exchanged[2 * bit], exchanged[2 * bit + 1], full[bit + 1]]
    (w,) = call(functools.partial(apex_kernel, low, depth), [tile], *above)
    incoming = w
    for mask in range(1, 1 << low):
        pairs = [(p, p + mask) for p in range(0, count_leaf, 1 << low)]
        copy = lax.ppermute(w, "leaf", pairs)
        incoming = jnp.where(position & ((1 << low) - 1) == mask, copy, incoming)
    (result,) = call(last_kernel, [rhs.shape], base, weight, incoming)
    return result


def call_tail(leaf_q, leaf_g, y, mid_q, mid_g, mid_y, pair_q, pair_g, pair_y, shape):
    leaves = leaf_q.shape[0]
    rank = pair_g.shape[2]
    operands = (leaf_q, leaf_g, y, mid_q, mid_g, mid_y, pair_q, pair_g, pair_y)
    outs = [jax.ShapeDtypeStruct(shape, F32), jax.ShapeDtypeStruct((shape[0], rank), F32)]
    size = sum(4 * a.size for a in operands + tuple(outs))
    return pl.pallas_call(
        tail_kernel,
        out_shape=outs,
        in_specs=[ANY, ANY] + [VMEM] * 7,
        out_specs=[VMEM, VMEM],
        scratch_shapes=[
            pltpu.VMEM(leaf_q.shape, F32),
            pltpu.VMEM(leaf_g.shape, F32),
            pltpu.SemaphoreType.DMA((2 * leaves,)),
        ],
        compiler_params=pltpu.CompilerParams(vmem_limit_bytes=40 * 2**20),
        cost_estimate=pl.CostEstimate(
            flops=8 * leaf_q.size * rank, bytes_accessed=size, transcendentals=0
        ),
    )(*operands)


def solution(mesh):
    both, chip = ("leaf", "panel"), "leaf"
    in_specs = (P(both, None),) + (P(both, None, None),) * 8 + (P(chip, None, None),) * 8
    return jax.shard_map(
        local, mesh=mesh, in_specs=in_specs, out_specs=P(both, None), check_vma=False
    )
```

```python
import functools

import jax
import jax.numpy as jnp
from jax import lax
from jax.experimental import pallas as pl
from jax.experimental.pallas import tpu as pltpu
from jax.sharding import PartitionSpec as P

F32 = jnp.float32
VMEM = pl.BlockSpec(memory_space=pltpu.VMEM)
ANY = pl.BlockSpec(memory_space=pl.ANY)
HBM = pl.BlockSpec(memory_space=pltpu.HBM)
NN = (((1,), (0,)), ((), ()))
NT = (((1,), (1,)), ((), ()))


def split(value):
    high = value.astype(jnp.bfloat16)
    return high, (value - high.astype(F32)).astype(jnp.bfloat16)


def product(left, right, dims):
    left_high, left_low = left if isinstance(left, tuple) else split(left)
    right_high, right_low = right if isinstance(right, tuple) else split(right)
    dot = functools.partial(lax.dot_general, dimension_numbers=dims, preferred_element_type=F32)
    return dot(left_high, right_high) + (dot(left_high, right_low) + dot(left_low, right_high))


def mm(left, right):
    return product(left, right, NN)


def mt(left, right):
    return product(left, right, NT)


STEP = 1 << 25


def call(kernel, outs, *operands, after=(), wait_in=(), alias=None, scratch=(), ahead=0):
    outs = [jax.ShapeDtypeStruct(shape, F32) for shape in outs]
    out_specs = [VMEM] * len(outs)
    aliases = {}
    wait_in = [pltpu.with_memory_space_constraint(a, pltpu.HBM) for a in wait_in]
    every = [*wait_in, *operands, *after]
    in_specs = [HBM] * len(wait_in) + [VMEM] * len(operands) + [ANY] * len(after)
    used = len(wait_in) + len(operands)
    if alias is not None:
        aliases[len(every)] = len(outs)
        every.append(alias)
        in_specs.append(ANY)
        outs.append(jax.ShapeDtypeStruct(alias.shape, F32))
        out_specs.append(ANY)
    n_in, n_out = len(every), len(outs) - len(aliases)

    def body(*refs):
        kernel(*refs[:used], *refs[n_in : n_in + n_out], *refs[n_in + len(outs) :])

    return pl.pallas_call(
        body,
        out_shape=outs,
        in_specs=in_specs,
        out_specs=out_specs,
        scratch_shapes=list(scratch),
        input_output_aliases=aliases,
        compiler_params=pltpu.CompilerParams(vmem_limit_bytes=20 * 2**20),
        cost_estimate=pl.CostEstimate(flops=0, bytes_accessed=ahead, transcendentals=0),
    )(*every)


def fetch(sources, targets, sems):
    copies = [
        pltpu.make_async_copy(s, t, sems.at[i]) for i, (s, t) in enumerate(zip(sources, targets))
    ]
    for copy in copies:
        copy.start()
    return copies


def up_rows(basis, inverse_factor, coupling_block, block_rows):
    e = inverse_factor.shape[0]
    c = mm(block_rows, basis)
    y = mt(c[:, :e], inverse_factor)
    return y, c[:, e:] - mt(y, coupling_block)


def node_kernel(q_h, e_h, f_h, g_h, low_ref, again_ref, high_ref, q_v, e_v, f_v, g_v, sems):
    rank = e_h.shape[1]
    copies = fetch(
        [f_h.at[0], e_h.at[0], q_h.at[0], g_h.at[0]], [f_v, e_v, q_v, g_v], sems
    )
    copies[0].wait()
    copies[1].wait()
    inverse = split(e_v[...])
    fe = mm(f_v[...], inverse)
    copies[2].wait()
    q = q_v[...]
    q1, q2 = split(q[:, :rank]), q[:, rank:]
    s = q2.T - mt(fe, q1)
    v = mm(q1, inverse)
    a = mt(v, q1)
    copies[3].wait()
    t = q2 - mm(q1, g_v[...])
    for half, ref in enumerate((low_ref, high_ref)):
        rows = slice(half * rank, (half + 1) * rank)
        ref[0] = s[:, :rank]
        ref[1] = s[:, rank:]
        ref[2] = a[rows, :rank]
        ref[3] = a[rows, rank:]
        ref[4] = t[rows]
    again_ref[...] = low_ref[...]

    @pl.when(lax.axis_index("leaf") == 0)
    def _():
        again_ref[4] = e_v[...]


def top_kernel(which, low_ref, high_ref, apex_ref, *out_refs):
    apex = split(apex_ref[4])
    s = [split(low_ref[0]), split(low_ref[1])]
    for half, out in zip(which, out_refs):
        ref = (low_ref, high_ref)[half]
        u = split(mm(ref[4], apex))
        out[0] = ref[2] + mm(u, s[0])
        out[1] = ref[3] + mm(u, s[1])


def choose(shape, choices, after=()):
    def kernel(*refs):
        position, core = lax.axis_index("leaf"), lax.axis_index("panel")
        out = refs[-1]
        for ref, (at_core, condition, _, start, count) in zip(refs, choices):
            here = condition(position)
            if at_core is not None:
                here = here & (core == at_core)

            def fill(ref=ref, start=start, count=count):
                out[0:count] = ref[start : start + count]

            pl.when(here)(fill)

    return call(kernel, [shape], *[c[2] for c in choices], after=after)[0]


def leaf_kernel(
    rhs, q, e, f, g, mid_q, mid_e, mid_f, mid_g, pair_q, pair_e, pair_f, pair_g,
    y_ref, mid_y_ref, z_ref, q_v, g_v, mid_q_v, mid_g_v,
    pair_q_v, pair_e_v, pair_f_v, pair_g_v, rhs_v, e_v, f_v, mid_e_v, mid_f_v, sems, later,
):
    leaves, size = q.shape[0], q.shape[1]
    sources, targets = [], []
    for n in range(leaves):
        rows = pl.ds(n * size, size)
        sources += [rhs.at[rows], q.at[n], e.at[n], f.at[n]]
        targets += [rhs_v.at[rows], q_v.at[n], e_v.at[n], f_v.at[n]]
    sources += [mid_q, mid_e, mid_f]
    targets += [mid_q_v, mid_e_v, mid_f_v]
    copies = fetch(sources, targets, sems)
    ahead = fetch(
        [pair_q, pair_e, pair_f, pair_g, mid_g, g],
        [pair_q_v, pair_e_v, pair_f_v, pair_g_v, mid_g_v, g_v],
        later,
    )
    reduced = []
    count = e.shape[1]
    for n in range(leaves):
        copies[4 * n].wait()
        block = rhs_v[n * size : (n + 1) * size, :].T
        copies[4 * n + 1].wait()
        c = mm(block, q_v[n])
        copies[4 * n + 2].wait()
        y = mt(c[:, :count], e_v[n])
        copies[4 * n + 3].wait()
        reduced.append(c[:, count:] - mt(y, f_v[n]))
        y_ref[n] = y
    for copy in copies[4 * leaves :]:
        copy.wait()
    y, z = up_rows(mid_q_v[0], mid_e_v[0], mid_f_v[0], jnp.concatenate(reduced, axis=1))
    mid_y_ref[...] = y
    z_ref[...] = z
    for copy in ahead:
        copy.wait()


def pair_kernel(own_ref, other_ref, q_ref, e_ref, f_ref, y_ref, z_ref):
    second = lax.axis_index("panel") == 1
    own, other = own_ref[...], other_ref[...]
    block = jnp.concatenate(
        [jnp.where(second, other, own), jnp.where(second, own, other)], axis=1
    )
    y, z = up_rows(q_ref[0], e_ref[0], f_ref[0], block)
    y_ref[...] = y
    z_ref[...] = z


def in_order(bit, own_ref, other_ref):
    second = (lax.axis_index("leaf") >> bit) & 1 == 1
    own, other = own_ref[...], other_ref[...]
    return jnp.where(second, other, own), jnp.where(second, own, other)


def level_kernel(bit, own_ref, other_ref, packet_ref, z_ref):
    first_z, second_z = in_order(bit, own_ref, other_ref)
    z_ref[...] = mt(first_z, packet_ref[0]) + mt(second_z, packet_ref[1])


def leaf_maps_kernel(q_ref, g_ref, y_ref, base_ref, t_ref):
    leaves, size = q_ref.shape[0], q_ref.shape[1]
    count = g_ref.shape[1]
    for n in range(leaves):
        q1 = split(q_ref[n, :, :count])
        rows = slice(n * size, (n + 1) * size)
        t_ref[rows] = q_ref[n, :, count:] - mm(q1, g_ref[n])
        base_ref[rows] = mt(q1, y_ref[n])


def fold_kernel(
    levels, base_ref, t_ref, mid_q_ref, mid_g_ref, mid_y_ref, pair_q_ref, pair_g_ref, pair_y_ref, *refs
):
    base_out, w_out = refs[-2:]
    rank = pair_g_ref.shape[2]
    start = lax.axis_index("panel") * rank
    pair_q = pair_q_ref[0, pl.ds(pl.multiple_of(start, rank), rank), :]
    pair_q1 = split(pair_q[:, :rank])
    pair_t = split(pair_q[:, rank:] - mm(pair_q1, pair_g_ref[0]))
    mid_q = mid_q_ref[0]
    mid_q1 = split(mid_q[:, :rank])
    mid_t = split(mid_q[:, rank:] - mm(mid_q1, mid_g_ref[0]))
    offset = chain = None
    for bit in range(levels):
        packet_ref = refs[3 * bit + 2]
        first_z, second_z = in_order(bit, *refs[3 * bit : 3 * bit + 2])
        u = mt(first_z, packet_ref[2]) + mt(second_z, packet_ref[3])
        if bit == 0:
            offset, chain = u, split(packet_ref[4])
        else:
            offset = offset + mt(u, chain)
            chain = split(mm(chain, packet_ref[4]))
    mid_w = mt(pair_y_ref[...], pair_q1)
    if chain is not None:
        mid_w = mid_w + mt(offset, pair_t)
        pair_t = split(mm(pair_t, chain))
    leaf_w = mt(mid_y_ref[...], mid_q1) + mt(mid_w, mid_t)
    map_w = mm(mid_t, pair_t)
    leaves = map_w.shape[0] // rank
    size = base_ref.shape[0] // leaves
    for n in range(leaves):
        rows = slice(n * size, (n + 1) * size)
        part = slice(n * rank, (n + 1) * rank)
        t = split(t_ref[rows])
        base_out[rows] = base_ref[rows] + mt(t, leaf_w[:, part])
        w_out[rows] = mm(t, map_w[part])


def apex_kernel(low, levels, *refs):
    out_ref = refs[-1]
    w = None
    for bit in range(levels - 1, low - 1, -1):
        packet_ref = refs[3 * (bit - low) + 2]
        first_z, second_z = in_order(bit, *refs[3 * (bit - low) : 3 * (bit - low) + 2])
        start = 0 if bit == levels - 1 else 2
        value = mt(first_z, packet_ref[start]) + mt(second_z, packet_ref[start + 1])
        if w is not None:
            value = value + mt(w, packet_ref[4])
        w = value
    out_ref[...] = w


def last_kernel(base_ref, w_ref, *refs):
    *incoming, out_ref = refs
    place = lax.axis_index("leaf") & (len(incoming) - 1)
    w = incoming[0][...]
    for mask in range(1, len(incoming)):
        w = jnp.where(place == mask, incoming[mask][...], w)
    out_ref[...] = base_ref[...] + mt(w_ref[...], w)


def home_core(level):
    return (0, 1, 1, 0)[(level - 1) % 4]


def lowest(bit):
    return lambda position: position & ((2 << bit) - 1) == 1 << bit


def clear(bits):
    return lambda position: position & ((1 << bits) - 1) == 0


def packet_rounds(depth, low):
    holders = {
        k: {(2 * j + 1) << (k - 1) for j in range(1 << (depth - k))} for k in range(1, depth + 1)
    }
    rounds = []
    for r in range(depth + 1):
        moves = []
        for level in range(1, depth + 1):
            bit = level - 1 - r + (level == depth)
            if bit == depth:
                moves.append((level, bit, [(0, 1 << (depth - 1))]))
            elif bit >= (0 if level <= low else low):
                pairs = [(p, p ^ (1 << bit)) for p in sorted(holders[level])]
                holders[level] |= {target for _, target in pairs}
                moves.append((level, bit, pairs))
        if moves:
            rounds.append(moves)
    return rounds


def local(
    rhs, leaf_q, leaf_e, leaf_f, leaf_g, mid_q, mid_e, mid_f, mid_g,
    pair_q, pair_e, pair_f, pair_g, up_q, up_e, up_f, up_g,
):
    count_leaf = lax.axis_size("leaf")
    cores = lax.axis_size("panel")
    depth = count_leaf.bit_length() - 1
    low = min(2, depth - 1)
    rank, columns = up_e.shape[1], rhs.shape[1]
    leaves, count = leaf_e.shape[0], leaf_e.shape[1]
    tile, packet = (columns, rank), (5, rank, rank)
    dma = pltpu.SemaphoreType.DMA

    def swap_cores(value):
        return lax.ppermute(value, "panel", [(i, cores - 1 - i) for i in range(cores)])

    def exchange(value, bit, step):
        pairs = [(p, p ^ (1 << bit)) for p in range(0, count_leaf, step)]
        return lax.ppermute(value, "leaf", pairs)

    low_half, low_again, high_half = call(
        node_kernel,
        [packet] * 3,
        wait_in=(up_q, up_e, up_f, up_g),
        scratch=[pltpu.VMEM(a.shape[1:], F32) for a in (up_q, up_e, up_f, up_g)] + [dma((4,))],
    )
    rounds = packet_rounds(depth, low)
    places = {k: [(lowest(k - 1), high_half, high_half, 0, 5)] for k in range(1, depth)}
    places[depth] = []
    top = {}

    def groups_of(index):
        lists = [[m for m in rounds[index] if home_core(m[0]) == c] for c in (0, 1)]
        longest = max(len(a) for a in lists)
        return [[a[i] for a in lists if i < len(a)] for i in range(longest)]

    def send(index, group, operand):
        pairs = []
        for level, _, moves in groups_of(index)[group]:
            c = home_core(level)
            pairs += [(p * cores + c, t * cores + c) for p, t in moves]
        return lax.ppermute(operand, ("leaf", "panel"), pairs)

    def blocks(level, index):
        return 2 if level == depth else 3 if level <= low and index > 0 else 5

    def operand_of(index, group):
        moves = groups_of(index)[group]
        choices = []
        for level, bit, _ in moves:
            c, n = home_core(level), blocks(level, index)
            if level == depth and bit == depth - 1:
                choices.append((c, lowest(bit), top["low"], 0, n))
                continue
            for condition, mine, _, start, held in places[level]:
                choices.append((c, condition, mine, start + held - n, n))
        size = max(blocks(level, index) for level, _, _ in moves)
        return choose((size, rank, rank), choices)

    def receive(index, group, incoming, after):
        incoming, _ = lax.optimization_barrier((incoming, after))
        other = swap_cores(incoming)
        for level, bit, _ in groups_of(index)[group]:
            if level == depth and bit == depth:
                top["mine"], top["other"] = incoming, other
                top["low"], top["high"] = call(
                    functools.partial(top_kernel, (0, 1)), [(2, rank, rank)] * 2,
                    low_half, high_half, incoming,
                )
                continue
            n = blocks(level, index)
            if index == 0 or (level == depth and bit == depth - 1):
                condition = clear(bit + 1)
            else:
                condition = lowest(bit)
            places[level].append((condition, incoming, other, 0, n))
        if any(level == depth and bit == depth for level, bit, _ in groups_of(index)[group]):
            places[depth].append((lowest(depth - 1), top["high"], None, 0, 2))

    def settle(level, after=()):
        c = home_core(level)
        choices = []
        size = packet if level < depth else (2, rank, rank)
        for condition, mine, other, start, n in places[level]:
            offset = size[0] - n if level < depth else 0
            if other is mine:
                choices.append((None, condition, mine, start, n, offset))
                continue
            choices.append((c, condition, mine, start, n, offset))
            if other is None:
                (other,) = call(
                    functools.partial(top_kernel, (1,)), [size], low_half, high_half, top["other"]
                )
            choices.append((cores - 1 - c, condition, other, start, n, offset))
        return place_blocks(size, choices, after)

    early = send(0, 0, low_half)

    wait_in = (
        rhs, leaf_q, leaf_e, leaf_f, leaf_g, mid_q, mid_e, mid_f, mid_g, pair_q, pair_e, pair_f, pair_g
    )
    kept = (leaf_q, leaf_g, mid_q, mid_g, pair_q, pair_e, pair_f, pair_g)
    y, mid_y, z, *kept = call(
        leaf_kernel,
        [(leaves, columns, count), tile, tile] + [a.shape for a in kept],
        wait_in=wait_in,
        ahead=STEP,
        scratch=[pltpu.VMEM(a.shape, F32) for a in (rhs, leaf_e, leaf_f, mid_e, mid_f)]
        + [dma((4 * leaves + 3,)), dma((6,))],
    )
    leaf_q, leaf_g, mid_q, mid_g, pair_q, pair_e, pair_f, pair_g = kept
    other = swap_cores(z)
    pair_y, z, low_again = call(
        pair_kernel, [tile, tile], z, other, pair_q, pair_e, pair_f, alias=low_again, ahead=STEP
    )
    flying = [(i, send(0, i, low_again)) for i in range(1, len(groups_of(0)))]

    exchanged, full = [], {}
    base = leaf_t = None

    def next_round(index, gate):
        for group, incoming in flying:
            receive(index, group, incoming, gate)
        flying.clear()
        if index + 1 < len(rounds):
            for group in range(len(groups_of(index + 1))):
                flying.append((group, send(index + 1, group, operand_of(index + 1, group))))

    for bit in range(depth):
        if bit == 0:
            receive(0, 0, early, z)
            full.update({level: settle(level) for level in range(1, low + 1)})
        else:
            next_round(bit - 1, z)
        if bit == 1:
            base, leaf_t = call(
                leaf_maps_kernel, [rhs.shape, (rhs.shape[0], rank)], leaf_q, leaf_g, y,
                after=(z,),
            )
        other = exchange(z, bit, 1 if bit < low else 1 << low)
        exchanged += [z, other]
        if bit < depth - 1:
            if bit >= low:
                full[bit + 1] = settle(bit + 1)
            (z,) = call(
                functools.partial(level_kernel, bit), [tile], z, other, full[bit + 1],
                after=(base,) if bit == 1 else (), ahead=STEP,
            )
    for index in range(depth - 1, len(rounds)):
        next_round(index, z)
    full[depth] = settle(depth)

    folded = []
    for bit in range(low):
        folded += [exchanged[2 * bit], exchanged[2 * bit + 1], settle(bit + 1) if bit else full[1]]
    base, weight = call(
        functools.partial(fold_kernel, low), [base.shape, leaf_t.shape], base, leaf_t,
        mid_q, mid_g, mid_y, pair_q, pair_g, pair_y, *folded,
    )

    above = []
    for bit in range(low, depth):
        above += [exchanged[2 * bit], exchanged[2 * bit + 1], full[bit + 1]]
    (w,) = call(
        functools.partial(apex_kernel, low, depth), [tile], *above, after=(base,), ahead=STEP
    )
    incoming = [w]
    for mask in range(1, 1 << low):
        pairs = [(p, p + mask) for p in range(0, count_leaf, 1 << low)]
        incoming.append(lax.ppermute(w, "leaf", pairs))
    (result,) = call(last_kernel, [rhs.shape], base, weight, *incoming)
    return result


def place_blocks(shape, choices, after):
    def kernel(*refs):
        position, core = lax.axis_index("leaf"), lax.axis_index("panel")
        out = refs[-1]
        for ref, (at_core, condition, _, start, count, offset) in zip(refs, choices):
            here = condition(position)
            if at_core is not None:
                here = here & (core == at_core)

            def fill(ref=ref, start=start, count=count, offset=offset):
                out[offset : offset + count] = ref[start : start + count]

            pl.when(here)(fill)

    return call(kernel, [shape], *[c[2] for c in choices], after=after)[0]


def solution(mesh):
    both, chip = ("leaf", "panel"), "leaf"
    in_specs = (P(both, None),) + (P(both, None, None),) * 8 + (P(chip, None, None),) * 8
    return jax.shard_map(
        local, mesh=mesh, in_specs=in_specs, out_specs=P(both, None), check_vma=False
    )
```

```python
import functools

import jax
import jax.numpy as jnp
from jax import lax
from jax.experimental import pallas as pl
from jax.experimental.pallas import tpu as pltpu
from jax.sharding import PartitionSpec as P

F32 = jnp.float32
VMEM = pl.BlockSpec(memory_space=pltpu.VMEM)
ANY = pl.BlockSpec(memory_space=pl.ANY)
HBM = pl.BlockSpec(memory_space=pltpu.HBM)
NN = (((1,), (0,)), ((), ()))
NT = (((1,), (1,)), ((), ()))


def split(value):
    high = value.astype(jnp.bfloat16)
    return high, (value - high.astype(F32)).astype(jnp.bfloat16)


def product(left, right, dims):
    left_high, left_low = left if isinstance(left, tuple) else split(left)
    right_high, right_low = right if isinstance(right, tuple) else split(right)
    dot = functools.partial(lax.dot_general, dimension_numbers=dims, preferred_element_type=F32)
    return dot(left_high, right_high) + (dot(left_high, right_low) + dot(left_low, right_high))


def mm(left, right):
    return product(left, right, NN)


def mt(left, right):
    return product(left, right, NT)


def call(kernel, outs, *operands, after=(), wait_in=(), through=(), scratch=(), cost=0):
    wait_in = [pltpu.with_memory_space_constraint(a, pltpu.HBM) for a in wait_in]
    used = len(wait_in) + len(operands)
    every = [*wait_in, *operands, *after, *through]
    out_shape = [jax.ShapeDtypeStruct(shape, F32) for shape in outs]
    out_shape += [jax.ShapeDtypeStruct(a.shape, F32) for a in through]
    n_in, n_out = len(every), len(outs)

    def body(*refs):
        kernel(*refs[:used], *refs[n_in : n_in + n_out], *refs[n_in + len(out_shape) :])

    return pl.pallas_call(
        body,
        out_shape=out_shape,
        in_specs=[HBM] * len(wait_in) + [VMEM] * len(operands) + [ANY] * (n_in - used),
        out_specs=[VMEM] * n_out + [ANY] * len(through),
        scratch_shapes=list(scratch),
        input_output_aliases={n_in - len(through) + i: n_out + i for i in range(len(through))},
        compiler_params=pltpu.CompilerParams(vmem_limit_bytes=20 * 2**20),
        cost_estimate=pl.CostEstimate(flops=cost, bytes_accessed=1000, transcendentals=0) if cost else None,
    )(*every)


def fetch(sources, targets, sems):
    copies = [
        pltpu.make_async_copy(s, t, sems.at[i]) for i, (s, t) in enumerate(zip(sources, targets))
    ]
    for copy in copies:
        copy.start()
    return copies


def up_rows(basis, inverse_factor, coupling_block, block_rows):
    e = inverse_factor.shape[0]
    c = mm(block_rows, basis)
    y = mt(c[:, :e], inverse_factor)
    return y, c[:, e:] - mt(y, coupling_block)


def node_maps(q, inverse, coupling, back, low_ref, high_ref):
    rank = back.shape[0]
    apex = inverse
    inverse = split(inverse)
    q1, q2 = split(q[:, :rank]), q[:, rank:]
    s = q2.T - mt(mm(coupling, inverse), q1)
    a = mt(mm(q1, inverse), q1)
    t = q2 - mm(q1, back)
    for half, ref in enumerate((low_ref, high_ref)):
        rows = slice(half * rank, (half + 1) * rank)
        ref[0] = s[:, :rank]
        ref[1] = s[:, rank:]
        ref[2] = a[rows, :rank]
        ref[3] = a[rows, rank:]
        ref[4] = t[rows]

    @pl.when(lax.axis_index("leaf") == 0)
    def _():
        low_ref[0] = apex


def node_kernel(
    up_q, up_e, up_f, up_g, low_ref, high_ref, up_q_v, up_e_v, up_f_v, up_g_v, sems
):
    for copy in fetch([up_q, up_e, up_f, up_g], [up_q_v, up_e_v, up_f_v, up_g_v], sems):
        copy.wait()
    node_maps(up_q_v[0], up_e_v[0], up_f_v[0], up_g_v[0], low_ref, high_ref)


def top_kernel(low_ref, high_ref, incoming_ref, out_ref):
    first = lax.axis_index("leaf") == 0
    apex = split(jnp.where(first, low_ref[0], incoming_ref[0]))

    def part(block):
        return jnp.where(first, incoming_ref[block], high_ref[block])

    u = split(mm(part(4), apex))
    out_ref[0] = part(2) + mm(u, part(0))
    out_ref[1] = part(3) + mm(u, part(1))


def choose(size, choices, after=()):
    def kernel(*refs):
        position, core = lax.axis_index("leaf"), lax.axis_index("panel")
        out = refs[-1]
        for ref, (at_core, condition, _, start, to, count) in zip(refs, choices):
            here = jnp.bool_(True) if condition is None else condition(position)
            if at_core is not None:
                here = here & (core == at_core)

            def fill(ref=ref, start=start, to=to, count=count):
                out[to : to + count] = ref[start : start + count]

            pl.when(here)(fill)

    shape = (size,) + choices[0][2].shape[1:]
    return call(kernel, [shape], *[c[2] for c in choices], after=after)[0]


def leaf_kernel(
    rhs, q, e, f, g, mid_q, mid_e, mid_f, mid_g, pair_q, pair_e, pair_f, pair_g,
    y_ref, mid_y_ref, z_ref, q_v, g_v, mid_q_v, mid_g_v, pair_q_v, pair_e_v, pair_f_v, pair_g_v,
    rhs_v, e_v, f_v, mid_e_v, mid_f_v, sems, later,
):
    leaves, size = q.shape[0], q.shape[1]
    sources, targets = [], []
    for n in range(leaves):
        rows = pl.ds(n * size, size)
        sources += [rhs.at[rows], q.at[n], e.at[n], f.at[n]]
        targets += [rhs_v.at[rows], q_v.at[n], e_v.at[n], f_v.at[n]]
    sources += [mid_q, mid_e, mid_f]
    targets += [mid_q_v, mid_e_v, mid_f_v]
    copies = fetch(sources, targets, sems)
    ahead = fetch(
        [pair_q, pair_e, pair_f, pair_g, mid_g, g],
        [pair_q_v, pair_e_v, pair_f_v, pair_g_v, mid_g_v, g_v],
        later,
    )
    reduced = []
    count = e.shape[1]
    for n in range(leaves):
        copies[4 * n].wait()
        block = rhs_v[n * size : (n + 1) * size, :].T
        copies[4 * n + 1].wait()
        c = mm(block, q_v[n])
        copies[4 * n + 2].wait()
        y = mt(c[:, :count], e_v[n])
        copies[4 * n + 3].wait()
        reduced.append(c[:, count:] - mt(y, f_v[n]))
        y_ref[n] = y
    for copy in copies[4 * leaves :]:
        copy.wait()
    y, z = up_rows(mid_q_v[0], mid_e_v[0], mid_f_v[0], jnp.concatenate(reduced, axis=1))
    mid_y_ref[...] = y
    z_ref[...] = z
    for copy in ahead:
        copy.wait()


def pair_kernel(own_ref, other_ref, q_ref, e_ref, f_ref, y_ref, z_ref):
    second = lax.axis_index("panel") == 1
    own, other = own_ref[...], other_ref[...]
    block = jnp.concatenate(
        [jnp.where(second, other, own), jnp.where(second, own, other)], axis=1
    )
    y, z = up_rows(q_ref[0], e_ref[0], f_ref[0], block)
    y_ref[...] = y
    z_ref[...] = z


def in_order(bit, own_ref, other_ref):
    second = (lax.axis_index("leaf") >> bit) & 1 == 1
    own, other = own_ref[...], other_ref[...]
    return jnp.where(second, other, own), jnp.where(second, own, other)


def level_kernel(bit, own_ref, other_ref, packet_ref, z_ref):
    first_z, second_z = in_order(bit, own_ref, other_ref)
    z_ref[...] = mt(first_z, packet_ref[0]) + mt(second_z, packet_ref[1])


def leaf_maps_kernel(q_ref, g_ref, y_ref, base_ref, t_ref):
    leaves, size = q_ref.shape[0], q_ref.shape[1]
    count = g_ref.shape[1]
    for n in range(leaves):
        q1 = split(q_ref[n, :, :count])
        rows = slice(n * size, (n + 1) * size)
        t_ref[rows] = q_ref[n, :, count:] - mm(q1, g_ref[n])
        base_ref[rows] = mt(q1, y_ref[n])


def fold_kernel(
    base_ref, t_ref, mid_q_ref, mid_g_ref, mid_y_ref, pair_q_ref, pair_g_ref, pair_y_ref, *refs
):
    *refs, base_out, w_out = refs
    rank = pair_g_ref.shape[2]
    start = lax.axis_index("panel") * rank
    pair_q = pair_q_ref[0, pl.ds(pl.multiple_of(start, rank), rank), :]
    pair_q1 = split(pair_q[:, :rank])
    pair_t = split(pair_q[:, rank:] - mm(pair_q1, pair_g_ref[0]))
    mid_q = mid_q_ref[0]
    mid_q1 = split(mid_q[:, :rank])
    mid_t = split(mid_q[:, rank:] - mm(mid_q1, mid_g_ref[0]))
    offset = chain = None
    for bit in range(len(refs) // 3):
        packet_ref = refs[3 * bit + 2]
        first_z, second_z = in_order(bit, *refs[3 * bit : 3 * bit + 2])
        u = mt(first_z, packet_ref[2]) + mt(second_z, packet_ref[3])
        if bit == 0:
            offset, chain = u, split(packet_ref[4])
        else:
            offset = offset + mt(u, chain)
            chain = split(mm(chain, packet_ref[4]))
    mid_w = mt(pair_y_ref[...], pair_q1) + mt(offset, pair_t)
    leaf_w = mt(mid_y_ref[...], mid_q1) + mt(mid_w, mid_t)
    map_w = mm(mid_t, mm(pair_t, chain))
    leaves = map_w.shape[0] // rank
    size = base_ref.shape[0] // leaves
    for n in range(leaves):
        rows = slice(n * size, (n + 1) * size)
        part = slice(n * rank, (n + 1) * rank)
        t = split(t_ref[rows])
        base_out[rows] = base_ref[rows] + mt(t, leaf_w[:, part])
        w_out[rows] = mm(t, map_w[part])


def last_kernel(low, levels, chunks, base_ref, weight_ref, *refs):
    *refs, out_ref, result, sems = refs
    w = None
    for bit in range(levels - 1, low - 1, -1):
        packet_ref = refs[3 * (bit - low) + 2]
        first_z, second_z = in_order(bit, *refs[3 * (bit - low) : 3 * (bit - low) + 2])
        start = 0 if bit == levels - 1 else 2
        value = mt(first_z, packet_ref[start]) + mt(second_z, packet_ref[start + 1])
        if w is not None:
            value = value + mt(w, packet_ref[4])
        w = value
    w = split(w)
    rows = result.shape[0] // chunks
    copies = []
    for i in range(chunks):
        part = pl.ds(i * rows, rows)
        result[part] = base_ref[part] + mt(weight_ref[part], w)
        copies.append(pltpu.make_async_copy(result.at[part], out_ref.at[part], sems.at[i]))
        copies[-1].start()
    for copy in copies:
        copy.wait()


def lowest(bit):
    return lambda position: position & ((2 << bit) - 1) == 1 << bit


def clear(bits):
    return lambda position: position & ((1 << bits) - 1) == 0


def local(
    rhs, leaf_q, leaf_e, leaf_f, leaf_g, mid_q, mid_e, mid_f, mid_g,
    pair_q, pair_e, pair_f, pair_g, up_q, up_e, up_f, up_g,
):
    count_leaf, cores = lax.axis_size("leaf"), lax.axis_size("panel")
    depth = count_leaf.bit_length() - 1
    assert depth > 2 and cores == 2
    folded = 2
    rank, columns = up_e.shape[1], rhs.shape[1]
    leaves, count = leaf_e.shape[0], leaf_e.shape[1]
    tile, packet, top_shape = (columns, rank), (5, rank, rank), (2, rank, rank)
    dma = pltpu.SemaphoreType.DMA

    def swap_cores(value):
        return lax.ppermute(value, "panel", [(i, cores - 1 - i) for i in range(cores)])

    def across(value, *masks):
        pairs = []
        for p in range(count_leaf):
            for c in range(cores):
                pairs.append((p * cores + c, (p ^ masks[c % len(masks)]) * cores + c))
        return lax.ppermute(value, ("leaf", "panel"), pairs)

    ups = (up_q, up_e, up_f, up_g)
    low_half, high_half = call(
        node_kernel,
        [packet] * 2,
        wait_in=ups,
        scratch=[pltpu.VMEM(a.shape, F32) for a in ups] + [dma((4,))],
    )

    def home(level):
        return (level - 1) % cores

    first_round = []
    for level in range(1, depth + 1, cores):
        masks = [1 << (k - 1) for k in range(level, min(level + cores, depth + 1))]
        first_round.append(across(low_half, *masks))

    wait_in = (
        rhs, leaf_q, leaf_e, leaf_f, leaf_g, mid_q, mid_e, mid_f, mid_g, pair_q, pair_e, pair_f, pair_g
    )
    kept = (leaf_q, leaf_g, mid_q, mid_g, pair_q, pair_e, pair_f, pair_g)
    y, mid_y, z, *kept = call(
        leaf_kernel,
        [(leaves, columns, count), tile, tile] + [a.shape for a in kept],
        wait_in=wait_in,
        scratch=[pltpu.VMEM(a.shape, F32) for a in (rhs, leaf_e, leaf_f, mid_e, mid_f)]
        + [dma((4 * leaves + 3,)), dma((6,))],
    )
    leaf_q, leaf_g, mid_q, mid_g, pair_q, pair_e, pair_f, pair_g = kept
    other = swap_cores(z)
    pair_y, z = call(pair_kernel, [tile, tile], z, other, pair_q, pair_e, pair_f)

    held, full = {}, {}

    def finish(level):
        c = home(level)
        swapped = swap_cores(held[level])
        n = held[level].shape[0]
        full[level] = choose(n, [(c, None, held[level], 0, 0, n), (1 - c, None, swapped, 0, 0, n)])

    def receive_first(gate):
        for level in range(1, depth + 1):
            incoming, _ = lax.optimization_barrier((first_round[(level - 1) // cores], gate))
            if level == depth:
                (held[level],) = call(top_kernel, [top_shape], low_half, high_half, incoming)
                continue
            held[level] = choose(
                5,
                [(None, lowest(level - 1), high_half, 0, 0, 5), (None, clear(level), incoming, 0, 0, 5)],
            )
        finish(1)

    def start_round(r):
        moves = [[], []]
        for level in range(max(r, 2), depth + 1):
            moves[home(level)].append((level, level - r))
        groups = []
        for i in range(max(len(side) for side in moves)):
            group = [side[i] for side in moves if i < len(side)]
            masks = [1 << group[0][1]] * cores
            size = max(held[level].shape[0] for level, _ in group)
            choices = []
            for level, bit in group:
                masks[home(level)] = 1 << bit
                choices.append((home(level), None, held[level], 0, 0, held[level].shape[0]))
            operand = held[group[0][0]] if len(group) == 1 else choose(size, choices)
            groups.append((group, across(operand, *masks)))
        return groups

    def receive(r, groups, gate):
        for group, incoming in groups:
            incoming, _ = lax.optimization_barrier((incoming, gate))
            for level, bit in group:
                before = held[level]
                n = before.shape[0]

                def stays(position, bit=bit):
                    return position & ((2 << bit) - 1) != 1 << bit

                value = choose(
                    n, [(None, stays, before, 0, 0, n), (None, lowest(bit), incoming, 0, 0, n)]
                )
                held[level] = value
                if bit == 0:
                    finish(level)

    exchanged = []
    flying = None
    base = weight = None
    for bit in range(depth):
        other = across(z, 1 << bit)
        exchanged += [(z, other)]
        if bit == 0:
            receive_first(z)
        else:
            receive(bit + 1, flying, z)
        if bit + 2 <= depth:
            flying = start_round(bit + 2)
        if bit == 1:
            base, leaf_t = call(
                leaf_maps_kernel, [rhs.shape, (rhs.shape[0], rank)], leaf_q, leaf_g, y, after=(z,)
            )
        if bit == depth - 1:
            lowest_levels = []
            for level in range(1, folded + 1):
                lowest_levels += [*exchanged[level - 1], full[level]]
            base, weight = call(
                fold_kernel, [base.shape, leaf_t.shape], base, leaf_t,
                mid_q, mid_g, mid_y, pair_q, pair_g, pair_y, *lowest_levels, after=(z,),
            )
            break
        (z,) = call(
            functools.partial(level_kernel, bit), [tile], z, other, full[bit + 1],
            after=() if bit != 1 else (base,), cost=500000000,
        )

    above = []
    for level in range(folded + 1, depth + 1):
        above += [*exchanged[level - 1], full[level]]
    chunks = 2 * leaves
    return last_step(
        functools.partial(last_kernel, folded, depth, chunks), rhs.shape, chunks, base, weight, *above
    )


def last_step(kernel, shape, chunks, *operands):
    return pl.pallas_call(
        kernel,
        out_shape=jax.ShapeDtypeStruct(shape, F32),
        in_specs=[VMEM] * len(operands),
        out_specs=HBM,
        scratch_shapes=[pltpu.VMEM(shape, F32), pltpu.SemaphoreType.DMA((chunks,))],
        compiler_params=pltpu.CompilerParams(vmem_limit_bytes=20 * 2**20),
    )(*operands)


def solution(mesh):
    both, chip = ("leaf", "panel"), "leaf"
    in_specs = (P(both, None),) + (P(both, None, None),) * 8 + (P(chip, None, None),) * 8
    return jax.shard_map(
        local, mesh=mesh, in_specs=in_specs, out_specs=P(both, None), check_vma=False
    )
```

```python
import functools

import jax
import jax.numpy as jnp
from jax import lax
from jax.experimental import pallas as pl
from jax.experimental.pallas import tpu as pltpu
from jax.sharding import PartitionSpec as P

F32 = jnp.float32
LV = (4000000000,4000000000,4000000000)+(500000000,)*9
VMEM = pl.BlockSpec(memory_space=pltpu.VMEM)
ANY = pl.BlockSpec(memory_space=pl.ANY)
HBM = pl.BlockSpec(memory_space=pltpu.HBM)
NN = (((1,), (0,)), ((), ()))
NT = (((1,), (1,)), ((), ()))


def split(value):
    high = value.astype(jnp.bfloat16)
    return high, (value - high.astype(F32)).astype(jnp.bfloat16)


def product(left, right, dims):
    left_high, left_low = left if isinstance(left, tuple) else split(left)
    right_high, right_low = right if isinstance(right, tuple) else split(right)
    dot = functools.partial(lax.dot_general, dimension_numbers=dims, preferred_element_type=F32)
    return dot(left_high, right_high) + (dot(left_high, right_low) + dot(left_low, right_high))


def mm(left, right):
    return product(left, right, NN)


def mt(left, right):
    return product(left, right, NT)


def call(kernel, outs, *operands, after=(), wait_in=(), through=(), scratch=(), cost=0):
    wait_in = [pltpu.with_memory_space_constraint(a, pltpu.HBM) for a in wait_in]
    used = len(wait_in) + len(operands)
    every = [*wait_in, *operands, *after, *through]
    out_shape = [jax.ShapeDtypeStruct(shape, F32) for shape in outs]
    out_shape += [jax.ShapeDtypeStruct(a.shape, F32) for a in through]
    n_in, n_out = len(every), len(outs)

    def body(*refs):
        kernel(*refs[:used], *refs[n_in : n_in + n_out], *refs[n_in + len(out_shape) :])

    return pl.pallas_call(
        body,
        name=getattr(kernel, "func", kernel).__name__,
        out_shape=out_shape,
        in_specs=[HBM] * len(wait_in) + [VMEM] * len(operands) + [ANY] * (n_in - used),
        out_specs=[VMEM] * n_out + [ANY] * len(through),
        scratch_shapes=list(scratch),
        input_output_aliases={n_in - len(through) + i: n_out + i for i in range(len(through))},
        compiler_params=pltpu.CompilerParams(vmem_limit_bytes=20 * 2**20),
        cost_estimate=pl.CostEstimate(flops=cost, bytes_accessed=1000, transcendentals=0) if cost else None,
    )(*every)


def fetch(sources, targets, sems):
    copies = [
        pltpu.make_async_copy(s, t, sems.at[i]) for i, (s, t) in enumerate(zip(sources, targets))
    ]
    for copy in copies:
        copy.start()
    return copies


def up_rows(basis, inverse_factor, coupling_block, block_rows):
    e = inverse_factor.shape[0]
    c = mm(block_rows, basis)
    y = mt(c[:, :e], inverse_factor)
    return y, c[:, e:] - mt(y, coupling_block)


def node_maps(q, inverse, coupling, back, low_ref, high_ref):
    rank = back.shape[0]
    apex = inverse
    inverse = split(inverse)
    q1, q2 = split(q[:, :rank]), q[:, rank:]
    s = q2.T - mt(mm(coupling, inverse), q1)
    a = mt(mm(q1, inverse), q1)
    t = q2 - mm(q1, back)
    for half, ref in enumerate((low_ref, high_ref)):
        rows = slice(half * rank, (half + 1) * rank)
        ref[0] = s[:, :rank]
        ref[1] = s[:, rank:]
        ref[2] = a[rows, :rank]
        ref[3] = a[rows, rank:]
        ref[4] = t[rows]

    @pl.when(lax.axis_index("leaf") == 0)
    def _():
        low_ref[0] = apex


def node_kernel(
    up_q, up_e, up_f, up_g, low_ref, high_ref, up_q_v, up_e_v, up_f_v, up_g_v, sems
):
    for copy in fetch([up_q, up_e, up_f, up_g], [up_q_v, up_e_v, up_f_v, up_g_v], sems):
        copy.wait()
    node_maps(up_q_v[0], up_e_v[0], up_f_v[0], up_g_v[0], low_ref, high_ref)


def top_kernel(low_ref, high_ref, incoming_ref, out_ref):
    first = lax.axis_index("leaf") == 0
    apex = split(jnp.where(first, low_ref[0], incoming_ref[0]))

    def part(block):
        return jnp.where(first, incoming_ref[block], high_ref[block])

    u = split(mm(part(4), apex))
    out_ref[0] = part(2) + mm(u, part(0))
    out_ref[1] = part(3) + mm(u, part(1))


def choose(size, choices, after=()):
    def kernel(*refs):
        position, core = lax.axis_index("leaf"), lax.axis_index("panel")
        out = refs[-1]
        for ref, (at_core, condition, _, start, to, count) in zip(refs, choices):
            here = jnp.bool_(True) if condition is None else condition(position)
            if at_core is not None:
                here = here & (core == at_core)

            def fill(ref=ref, start=start, to=to, count=count):
                out[to : to + count] = ref[start : start + count]

            pl.when(here)(fill)

    shape = (size,) + choices[0][2].shape[1:]
    return call(kernel, [shape], *[c[2] for c in choices], after=after, cost=1000)[0]


def leaf_kernel(
    rhs, q, e, f, g, mid_q, mid_e, mid_f, mid_g, pair_q, pair_e, pair_f, pair_g,
    y_ref, mid_y_ref, z_ref, q_v, g_v, mid_q_v, mid_g_v, pair_q_v, pair_e_v, pair_f_v, pair_g_v,
    rhs_v, e_v, f_v, mid_e_v, mid_f_v, sems, later,
):
    leaves, size = q.shape[0], q.shape[1]
    sources, targets = [], []
    for n in range(leaves):
        rows = pl.ds(n * size, size)
        sources += [rhs.at[rows], q.at[n], e.at[n], f.at[n]]
        targets += [rhs_v.at[rows], q_v.at[n], e_v.at[n], f_v.at[n]]
    sources += [mid_q, mid_e, mid_f]
    targets += [mid_q_v, mid_e_v, mid_f_v]
    copies = fetch(sources, targets, sems)
    ahead = fetch(
        [pair_q, pair_e, pair_f, pair_g, mid_g, g],
        [pair_q_v, pair_e_v, pair_f_v, pair_g_v, mid_g_v, g_v],
        later,
    )
    reduced = []
    count = e.shape[1]
    for n in range(leaves):
        copies[4 * n].wait()
        block = rhs_v[n * size : (n + 1) * size, :].T
        copies[4 * n + 1].wait()
        c = mm(block, q_v[n])
        copies[4 * n + 2].wait()
        y = mt(c[:, :count], e_v[n])
        copies[4 * n + 3].wait()
        reduced.append(c[:, count:] - mt(y, f_v[n]))
        y_ref[n] = y
    for copy in copies[4 * leaves :]:
        copy.wait()
    y, z = up_rows(mid_q_v[0], mid_e_v[0], mid_f_v[0], jnp.concatenate(reduced, axis=1))
    mid_y_ref[...] = y
    z_ref[...] = z
    for copy in ahead:
        copy.wait()


def pair_kernel(own_ref, other_ref, q_ref, e_ref, f_ref, y_ref, z_ref):
    second = lax.axis_index("panel") == 1
    own, other = own_ref[...], other_ref[...]
    block = jnp.concatenate(
        [jnp.where(second, other, own), jnp.where(second, own, other)], axis=1
    )
    y, z = up_rows(q_ref[0], e_ref[0], f_ref[0], block)
    y_ref[...] = y
    z_ref[...] = z


def mark_kernel(ref, out_ref):
    out_ref[...] = ref[: out_ref.shape[0]]


def in_order(bit, own_ref, other_ref):
    second = (lax.axis_index("leaf") >> bit) & 1 == 1
    own, other = own_ref[...], other_ref[...]
    return jnp.where(second, other, own), jnp.where(second, own, other)


def level_kernel(bit, own_ref, other_ref, packet_ref, z_ref):
    first_z, second_z = in_order(bit, own_ref, other_ref)
    z_ref[...] = mt(first_z, packet_ref[0]) + mt(second_z, packet_ref[1])


def leaf_maps_kernel(q_ref, g_ref, y_ref, base_ref, t_ref):
    leaves, size = q_ref.shape[0], q_ref.shape[1]
    count = g_ref.shape[1]
    for n in range(leaves):
        q1 = split(q_ref[n, :, :count])
        rows = slice(n * size, (n + 1) * size)
        t_ref[rows] = q_ref[n, :, count:] - mm(q1, g_ref[n])
        base_ref[rows] = mt(q1, y_ref[n])


def fold_kernel(
    base_ref, t_ref, mid_q_ref, mid_g_ref, mid_y_ref, pair_q_ref, pair_g_ref, pair_y_ref, *refs
):
    *refs, base_out, w_out = refs
    rank = pair_g_ref.shape[2]
    start = lax.axis_index("panel") * rank
    pair_q = pair_q_ref[0, pl.ds(pl.multiple_of(start, rank), rank), :]
    pair_q1 = split(pair_q[:, :rank])
    pair_t = split(pair_q[:, rank:] - mm(pair_q1, pair_g_ref[0]))
    mid_q = mid_q_ref[0]
    mid_q1 = split(mid_q[:, :rank])
    mid_t = split(mid_q[:, rank:] - mm(mid_q1, mid_g_ref[0]))
    offset = chain = None
    for bit in range(len(refs) // 3):
        packet_ref = refs[3 * bit + 2]
        first_z, second_z = in_order(bit, *refs[3 * bit : 3 * bit + 2])
        u = mt(first_z, packet_ref[0]) + mt(second_z, packet_ref[1])
        if bit == 0:
            offset, chain = u, split(packet_ref[2])
        else:
            offset = offset + mt(u, chain)
            chain = split(mm(chain, packet_ref[2]))
    mid_w = mt(pair_y_ref[...], pair_q1) + mt(offset, pair_t)
    leaf_w = mt(mid_y_ref[...], mid_q1) + mt(mid_w, mid_t)
    map_w = mm(mid_t, mm(pair_t, chain))
    leaves = map_w.shape[0] // rank
    size = base_ref.shape[0] // leaves
    for n in range(leaves):
        rows = slice(n * size, (n + 1) * size)
        part = slice(n * rank, (n + 1) * rank)
        t = split(t_ref[rows])
        base_out[rows] = base_ref[rows] + mt(t, leaf_w[:, part])
        w_out[rows] = mm(t, map_w[part])


def last_kernel(bit, chunks, base_ref, weight_ref, own_ref, other_ref, top_ref, out_ref, result, sems):
    first_z, second_z = in_order(bit, own_ref, other_ref)
    w = mt(first_z, top_ref[0]) + mt(second_z, top_ref[1])
    w = split(w)
    rows = result.shape[0] // chunks
    copies = []
    for i in range(chunks):
        part = pl.ds(i * rows, rows)
        result[part] = base_ref[part] + mt(weight_ref[part], w)
        copies.append(pltpu.make_async_copy(result.at[part], out_ref.at[part], sems.at[i]))
        copies[-1].start()
    for copy in copies:
        copy.wait()


def lowest(bit):
    return lambda position: position & ((2 << bit) - 1) == 1 << bit


def clear(bits):
    return lambda position: position & ((1 << bits) - 1) == 0


def local(
    rhs, leaf_q, leaf_e, leaf_f, leaf_g, mid_q, mid_e, mid_f, mid_g,
    pair_q, pair_e, pair_f, pair_g, up_q, up_e, up_f, up_g,
):
    count_leaf, cores = lax.axis_size("leaf"), lax.axis_size("panel")
    depth = count_leaf.bit_length() - 1
    assert depth > 2 and cores == 2
    rank, columns = up_e.shape[1], rhs.shape[1]
    leaves, count = leaf_e.shape[0], leaf_e.shape[1]
    tile, packet, top_shape = (columns, rank), (5, rank, rank), (2, rank, rank)
    dma = pltpu.SemaphoreType.DMA

    def swap_cores(value):
        return lax.ppermute(value, "panel", [(i, cores - 1 - i) for i in range(cores)])

    def across(value, *masks):
        pairs = []
        for p in range(count_leaf):
            for c in range(cores):
                pairs.append((p * cores + c, (p ^ masks[c % len(masks)]) * cores + c))
        return lax.ppermute(value, ("leaf", "panel"), pairs)

    ups = (up_q, up_e, up_f, up_g)
    low_half, high_half = call(
        node_kernel,
        [packet] * 2,
        wait_in=ups,
        scratch=[pltpu.VMEM(a.shape, F32) for a in ups] + [dma((4,))],
    )

    def home(level):
        return (level - 1) % cores

    sides = [[k for k in range(1, depth + 1) if home(k) == c] for c in range(cores)]
    sides[1].reverse()
    first_round = {}
    for i, level in enumerate(sides[0]):
        pair = [level, *sides[1][i : i + 1]]
        incoming = across(low_half, *[1 << (k - 1) for k in pair])
        first_round.update({k: incoming for k in pair})

    wait_in = (
        rhs, leaf_q, leaf_e, leaf_f, leaf_g, mid_q, mid_e, mid_f, mid_g, pair_q, pair_e, pair_f, pair_g
    )
    kept = (leaf_q, leaf_g, mid_q, mid_g, pair_q, pair_e, pair_f, pair_g)
    y, mid_y, z, *kept = call(
        leaf_kernel,
        [(leaves, columns, count), tile, tile] + [a.shape for a in kept],
        wait_in=wait_in,
        scratch=[pltpu.VMEM(a.shape, F32) for a in (rhs, leaf_e, leaf_f, mid_e, mid_f)]
        + [dma((4 * leaves + 3,)), dma((6,))],
        cost=1000,
    )
    leaf_q, leaf_g, mid_q, mid_g, pair_q, pair_e, pair_f, pair_g = kept
    other = swap_cores(z)
    base, leaf_t = call(
        leaf_maps_kernel, [rhs.shape, (rhs.shape[0], rank)], leaf_q, leaf_g, y, cost=1000000000
    )
    pair_y, z = call(
        pair_kernel, [tile, tile], z, other, pair_q, pair_e, pair_f, after=(base,), cost=1000
    )

    up, down, full_up, full_down = {}, {}, {}, {}

    def on_both(level, here, after=()):
        c, n = home(level), here.shape[0]
        swapped = swap_cores(here)
        return choose(n, [(c, None, here, 0, 0, n), (1 - c, None, swapped, 0, 0, n)], after=after)

    def receive_first(gate):
        for level in range(1, depth + 1):
            incoming, _ = lax.optimization_barrier((first_round[level], gate))
            if level == depth:
                (up[level],) = call(top_kernel, [top_shape], low_half, high_half, incoming, cost=1000)
                continue
            owner, below = lowest(level - 1), clear(level)
            for held, first, n in ((up, 0, 2), (down, 2, 3)):
                held[level] = choose(
                    n, [(None, owner, high_half, first, 0, n), (None, below, incoming, first, 0, n)]
                )
        full_up[1], full_down[1] = on_both(1, up[1]), on_both(1, down[1])

    def start_round(r, held):
        moves = [[], []]
        for level in range(max(r, 2), depth + 1):
            if level in held:
                moves[home(level)].append((level, level - r))
        groups = []
        for i in range(max(len(side) for side in moves)):
            group = [side[i] for side in moves if i < len(side)]
            masks = [1 << (group[0][1] != 1)] * cores
            choices = []
            for level, bit in group:
                masks[home(level)] = 1 << bit
                choices.append((home(level), None, held[level], 0, 0, held[level].shape[0]))
            n = held[group[0][0]].shape[0]
            operand = held[group[0][0]] if len(group) == 1 else choose(n, choices)
            groups.append((group, across(operand, *masks)))
        return groups

    def receive(groups, held, full, gate, after=()):
        for group, incoming in groups:
            incoming, _ = lax.optimization_barrier((incoming, gate))
            for level, bit in group:
                before = held[level]
                n = before.shape[0]

                def stays(position, bit=bit):
                    return position & ((2 << bit) - 1) != 1 << bit

                held[level] = choose(
                    n, [(None, stays, before, 0, 0, n), (None, lowest(bit), incoming, 0, 0, n)]
                )
                if bit == 0:
                    full[level] = on_both(level, held[level], after)

    exchanged = []
    flying_up = flying_down = ()
    for bit in range(depth):
        other = across(z, 1 << bit)
        exchanged += [(z, other)]
        if bit == 0:
            receive_first(z)
        mark = call(mark_kernel, [(8, rank)], z, cost=4000000000)
        if bit != depth - 2:
            receive(flying_down, down, full_down, z, mark)
        if bit == depth - 1:
            lowest_levels = []
            for level in range(1, depth):
                lowest_levels += [*exchanged[level - 1], full_down[level]]
            base, weight = call(
                fold_kernel, [base.shape, leaf_t.shape], base, leaf_t,
                mid_q, mid_g, mid_y, pair_q, pair_g, pair_y, *lowest_levels, after=(z,), cost=2000000000,
            )
            receive(flying_up, up, full_up, z, (weight,))
            break
        receive(flying_up, up, full_up, z, mark)
        flying_up = start_round(bit + 2, up) if bit + 2 <= depth else ()
        if bit + 2 < depth:
            flying_down = start_round(bit + 2, down)
        (z,) = call(
            functools.partial(level_kernel, bit), [tile], z, other, full_up[bit + 1],
            cost=LV[bit],
        )

    chunks = 2 * leaves
    return last_step(
        functools.partial(last_kernel, depth - 1, chunks), rhs.shape, chunks, base, weight,
        *exchanged[depth - 1], full_up[depth],
    )


def last_step(kernel, shape, chunks, *operands):
    return pl.pallas_call(
        kernel,
        out_shape=jax.ShapeDtypeStruct(shape, F32),
        in_specs=[VMEM] * len(operands),
        out_specs=HBM,
        scratch_shapes=[pltpu.VMEM(shape, F32), pltpu.SemaphoreType.DMA((chunks,))],
        compiler_params=pltpu.CompilerParams(vmem_limit_bytes=20 * 2**20),
    )(*operands)


def solution(mesh):
    both, chip = ("leaf", "panel"), "leaf"
    in_specs = (P(both, None),) + (P(both, None, None),) * 8 + (P(chip, None, None),) * 8
    return jax.shard_map(
        local, mesh=mesh, in_specs=in_specs, out_specs=P(both, None), check_vma=False
    )
```

```python
import functools

import jax
import jax.numpy as jnp
from jax import lax
from jax.experimental import pallas as pl
from jax.experimental.pallas import tpu as pltpu
from jax.sharding import PartitionSpec as P

F32 = jnp.float32
LV = (4000000000,4000000000,4000000000)+(500000000,)*9
VMEM = pl.BlockSpec(memory_space=pltpu.VMEM)
ANY = pl.BlockSpec(memory_space=pl.ANY)
HBM = pl.BlockSpec(memory_space=pltpu.HBM)
NN = (((1,), (0,)), ((), ()))
NT = (((1,), (1,)), ((), ()))


def split(value):
    high = value.astype(jnp.bfloat16)
    return high, (value - high.astype(F32)).astype(jnp.bfloat16)


def product(left, right, dims):
    left_high, left_low = left if isinstance(left, tuple) else split(left)
    right_high, right_low = right if isinstance(right, tuple) else split(right)
    dot = functools.partial(lax.dot_general, dimension_numbers=dims, preferred_element_type=F32)
    if left_high.shape[0] <= right_high.shape[1 - dims[0][1][0]]:
        axis = dims[0][1][0]
        return dot(
            jnp.concatenate([left_high, left_high, left_low], axis=1),
            jnp.concatenate([right_high, right_low, right_high], axis=axis),
        )
    return dot(left_high, right_high) + (dot(left_high, right_low) + dot(left_low, right_high))


def mm(left, right):
    return product(left, right, NN)


def mt(left, right):
    return product(left, right, NT)


def call(kernel, outs, *operands, after=(), wait_in=(), through=(), scratch=(), cost=0):
    wait_in = [pltpu.with_memory_space_constraint(a, pltpu.HBM) for a in wait_in]
    used = len(wait_in) + len(operands)
    every = [*wait_in, *operands, *after, *through]
    out_shape = [jax.ShapeDtypeStruct(shape, F32) for shape in outs]
    out_shape += [jax.ShapeDtypeStruct(a.shape, F32) for a in through]
    n_in, n_out = len(every), len(outs)

    def body(*refs):
        kernel(*refs[:used], *refs[n_in : n_in + n_out], *refs[n_in + len(out_shape) :])

    return pl.pallas_call(
        body,
        name=getattr(kernel, "func", kernel).__name__,
        out_shape=out_shape,
        in_specs=[HBM] * len(wait_in) + [VMEM] * len(operands) + [ANY] * (n_in - used),
        out_specs=[VMEM] * n_out + [ANY] * len(through),
        scratch_shapes=list(scratch),
        input_output_aliases={n_in - len(through) + i: n_out + i for i in range(len(through))},
        compiler_params=pltpu.CompilerParams(vmem_limit_bytes=20 * 2**20),
        cost_estimate=pl.CostEstimate(flops=cost, bytes_accessed=1000, transcendentals=0) if cost else None,
    )(*every)


def fetch(sources, targets, sems):
    copies = [
        pltpu.make_async_copy(s, t, sems.at[i]) for i, (s, t) in enumerate(zip(sources, targets))
    ]
    for copy in copies:
        copy.start()
    return copies


def up_rows(basis, inverse_factor, coupling_block, block_rows):
    e = inverse_factor.shape[0]
    c = mm(block_rows, basis)
    y = mt(c[:, :e], inverse_factor)
    return y, c[:, e:] - mt(y, coupling_block)


def node_maps(q, inverse, coupling, back, low_ref, high_ref):
    rank = back.shape[0]
    apex = inverse
    inverse = split(inverse)
    q1, q2 = split(q[:, :rank]), q[:, rank:]
    s = q2.T - mt(mm(coupling, inverse), q1)
    a = mt(mm(q1, inverse), q1)
    t = q2 - mm(q1, back)
    for half, ref in enumerate((low_ref, high_ref)):
        rows = slice(half * rank, (half + 1) * rank)
        ref[0] = s[:, :rank]
        ref[1] = s[:, rank:]
        ref[2] = a[rows, :rank]
        ref[3] = a[rows, rank:]
        ref[4] = t[rows]

    @pl.when(lax.axis_index("leaf") == 0)
    def _():
        low_ref[0] = apex


def node_kernel(
    up_q, up_e, up_f, up_g, low_ref, high_ref, up_q_v, up_e_v, up_f_v, up_g_v, sems
):
    for copy in fetch([up_q, up_e, up_f, up_g], [up_q_v, up_e_v, up_f_v, up_g_v], sems):
        copy.wait()
    node_maps(up_q_v[0], up_e_v[0], up_f_v[0], up_g_v[0], low_ref, high_ref)


def top_kernel(low_ref, high_ref, incoming_ref, out_ref):
    first = lax.axis_index("leaf") == 0
    apex = split(jnp.where(first, low_ref[0], incoming_ref[0]))

    def part(block):
        return jnp.where(first, incoming_ref[block], high_ref[block])

    u = split(mm(part(4), apex))
    out_ref[0] = part(2) + mm(u, part(0))
    out_ref[1] = part(3) + mm(u, part(1))


def choose(size, choices, after=()):
    def kernel(*refs):
        position, core = lax.axis_index("leaf"), lax.axis_index("panel")
        out = refs[-1]
        for ref, (at_core, condition, _, start, to, count) in zip(refs, choices):
            here = jnp.bool_(True) if condition is None else condition(position)
            if at_core is not None:
                here = here & (core == at_core)

            def fill(ref=ref, start=start, to=to, count=count):
                out[to : to + count] = ref[start : start + count]

            pl.when(here)(fill)

    shape = (size,) + choices[0][2].shape[1:]
    return call(kernel, [shape], *[c[2] for c in choices], after=after, cost=1000)[0]


def leaf_kernel(
    rhs, q, e, f, g, mid_q, mid_e, mid_f, mid_g, pair_q, pair_e, pair_f, pair_g,
    y_ref, mid_y_ref, z_ref, q_v, g_v, mid_q_v, mid_g_v, pair_q_v, pair_e_v, pair_f_v, pair_g_v,
    rhs_v, e_v, f_v, mid_e_v, mid_f_v, sems, later,
):
    leaves, size = q.shape[0], q.shape[1]
    sources, targets = [], []
    for n in range(leaves):
        rows = pl.ds(n * size, size)
        sources += [rhs.at[rows], q.at[n], e.at[n], f.at[n]]
        targets += [rhs_v.at[rows], q_v.at[n], e_v.at[n], f_v.at[n]]
    sources += [mid_q, mid_e, mid_f]
    targets += [mid_q_v, mid_e_v, mid_f_v]
    copies = fetch(sources, targets, sems)
    reduced = []
    count = e.shape[1]
    for n in range(leaves):
        copies[4 * n].wait()
        block = rhs_v[n * size : (n + 1) * size, :].T
        copies[4 * n + 1].wait()
        if n == 0:
            ahead = fetch(
                [pair_q, pair_e, pair_f, pair_g, mid_g, g],
                [pair_q_v, pair_e_v, pair_f_v, pair_g_v, mid_g_v, g_v],
                later,
            )
        c = mm(block, q_v[n])
        copies[4 * n + 2].wait()
        y = mt(c[:, :count], e_v[n])
        copies[4 * n + 3].wait()
        reduced.append(c[:, count:] - mt(y, f_v[n]))
        y_ref[n] = y
    for copy in copies[4 * leaves :]:
        copy.wait()
    y, z = up_rows(mid_q_v[0], mid_e_v[0], mid_f_v[0], jnp.concatenate(reduced, axis=1))
    mid_y_ref[...] = y
    z_ref[...] = z
    for copy in ahead:
        copy.wait()


def pair_kernel(own_ref, other_ref, q_ref, e_ref, f_ref, y_ref, z_ref):
    second = lax.axis_index("panel") == 1
    own, other = own_ref[...], other_ref[...]
    block = jnp.concatenate(
        [jnp.where(second, other, own), jnp.where(second, own, other)], axis=1
    )
    y, z = up_rows(q_ref[0], e_ref[0], f_ref[0], block)
    y_ref[...] = y
    z_ref[...] = z


def mark_kernel(ref, out_ref):
    out_ref[...] = ref[: out_ref.shape[0]]


def in_order(bit, own_ref, other_ref):
    second = (lax.axis_index("leaf") >> bit) & 1 == 1
    own, other = own_ref[...], other_ref[...]
    return jnp.where(second, other, own), jnp.where(second, own, other)


def level_kernel(bit, own_ref, other_ref, packet_ref, z_ref):
    first_z, second_z = in_order(bit, own_ref, other_ref)
    z_ref[...] = mt(first_z, packet_ref[0]) + mt(second_z, packet_ref[1])


def leaf_maps_kernel(q_ref, g_ref, y_ref, base_ref, t_ref):
    leaves, size = q_ref.shape[0], q_ref.shape[1]
    count = g_ref.shape[1]
    for n in range(leaves):
        q1 = split(q_ref[n, :, :count])
        rows = slice(n * size, (n + 1) * size)
        t_ref[rows] = q_ref[n, :, count:] - mm(q1, g_ref[n])
        base_ref[rows] = mt(q1, y_ref[n])


def fold_kernel(
    base_ref, t_ref, mid_q_ref, mid_g_ref, mid_y_ref, pair_q_ref, pair_g_ref, pair_y_ref, *refs
):
    *refs, base_out, w_out = refs
    rank = pair_g_ref.shape[2]
    start = lax.axis_index("panel") * rank
    pair_q = pair_q_ref[0, pl.ds(pl.multiple_of(start, rank), rank), :]
    pair_q1 = split(pair_q[:, :rank])
    pair_t = split(pair_q[:, rank:] - mm(pair_q1, pair_g_ref[0]))
    mid_q = mid_q_ref[0]
    mid_q1 = split(mid_q[:, :rank])
    mid_t = split(mid_q[:, rank:] - mm(mid_q1, mid_g_ref[0]))
    offset = chain = None
    for bit in range(len(refs) // 3):
        packet_ref = refs[3 * bit + 2]
        first_z, second_z = in_order(bit, *refs[3 * bit : 3 * bit + 2])
        u = mt(first_z, packet_ref[0]) + mt(second_z, packet_ref[1])
        if bit == 0:
            offset, chain = u, split(packet_ref[2])
        else:
            offset = offset + mt(u, chain)
            chain = split(mm(chain, packet_ref[2]))
    mid_w = mt(pair_y_ref[...], pair_q1) + mt(offset, pair_t)
    leaf_w = mt(mid_y_ref[...], mid_q1) + mt(mid_w, mid_t)
    map_w = mm(mid_t, mm(pair_t, chain))
    leaves = map_w.shape[0] // rank
    size = base_ref.shape[0] // leaves
    for n in range(leaves):
        rows = slice(n * size, (n + 1) * size)
        part = slice(n * rank, (n + 1) * rank)
        t = split(t_ref[rows])
        base_out[rows] = base_ref[rows] + mt(t, leaf_w[:, part])
        w_out[rows] = mm(t, map_w[part])


def last_kernel(bit, chunks, base_ref, weight_ref, own_ref, other_ref, top_ref, out_ref, result, sems):
    first_z, second_z = in_order(bit, own_ref, other_ref)
    w = mt(first_z, top_ref[0]) + mt(second_z, top_ref[1])
    w = split(w)
    rows = result.shape[0] // chunks
    copies = []
    for i in range(chunks):
        part = pl.ds(i * rows, rows)
        result[part] = base_ref[part] + mt(weight_ref[part], w)
        copies.append(pltpu.make_async_copy(result.at[part], out_ref.at[part], sems.at[i]))
        copies[-1].start()
    for copy in copies:
        copy.wait()


def lowest(bit):
    return lambda position: position & ((2 << bit) - 1) == 1 << bit


def clear(bits):
    return lambda position: position & ((1 << bits) - 1) == 0


def local(
    rhs, leaf_q, leaf_e, leaf_f, leaf_g, mid_q, mid_e, mid_f, mid_g,
    pair_q, pair_e, pair_f, pair_g, up_q, up_e, up_f, up_g,
):
    count_leaf, cores = lax.axis_size("leaf"), lax.axis_size("panel")
    depth = count_leaf.bit_length() - 1
    assert depth > 2 and cores == 2
    rank, columns = up_e.shape[1], rhs.shape[1]
    leaves, count = leaf_e.shape[0], leaf_e.shape[1]
    tile, packet, top_shape = (columns, rank), (5, rank, rank), (2, rank, rank)
    dma = pltpu.SemaphoreType.DMA

    def swap_cores(value):
        return lax.ppermute(value, "panel", [(i, cores - 1 - i) for i in range(cores)])

    def across(value, *masks):
        pairs = []
        for p in range(count_leaf):
            for c in range(cores):
                pairs.append((p * cores + c, (p ^ masks[c % len(masks)]) * cores + c))
        return lax.ppermute(value, ("leaf", "panel"), pairs)

    ups = (up_q, up_e, up_f, up_g)
    low_half, high_half = call(
        node_kernel,
        [packet] * 2,
        wait_in=ups,
        scratch=[pltpu.VMEM(a.shape, F32) for a in ups] + [dma((4,))],
    )

    def home(level):
        return (level - 1) % cores

    sides = [[k for k in range(1, depth + 1) if home(k) == c] for c in range(cores)]
    sides[1].reverse()
    first_round = {}
    for i, level in enumerate(sides[0]):
        pair = [level, *sides[1][i : i + 1]]
        incoming = across(low_half, *[1 << (k - 1) for k in pair])
        first_round.update({k: incoming for k in pair})

    wait_in = (
        rhs, leaf_q, leaf_e, leaf_f, leaf_g, mid_q, mid_e, mid_f, mid_g, pair_q, pair_e, pair_f, pair_g
    )
    kept = (leaf_q, leaf_g, mid_q, mid_g, pair_q, pair_e, pair_f, pair_g)
    y, mid_y, z, *kept = call(
        leaf_kernel,
        [(leaves, columns, count), tile, tile] + [a.shape for a in kept],
        wait_in=wait_in,
        scratch=[pltpu.VMEM(a.shape, F32) for a in (rhs, leaf_e, leaf_f, mid_e, mid_f)]
        + [dma((4 * leaves + 3,)), dma((6,))],
        cost=1000,
    )
    leaf_q, leaf_g, mid_q, mid_g, pair_q, pair_e, pair_f, pair_g = kept
    other = swap_cores(z)
    base, leaf_t = call(
        leaf_maps_kernel, [rhs.shape, (rhs.shape[0], rank)], leaf_q, leaf_g, y, cost=1000000000
    )
    pair_y, z = call(
        pair_kernel, [tile, tile], z, other, pair_q, pair_e, pair_f, after=(base,), cost=1000
    )

    up, down, full_up, full_down = {}, {}, {}, {}

    def on_both(level, here, after=()):
        c, n = home(level), here.shape[0]
        swapped = swap_cores(here)
        return choose(n, [(c, None, here, 0, 0, n), (1 - c, None, swapped, 0, 0, n)], after=after)

    def receive_first(gate):
        for level in range(1, depth + 1):
            incoming, _ = lax.optimization_barrier((first_round[level], gate))
            if level == depth:
                (up[level],) = call(top_kernel, [top_shape], low_half, high_half, incoming, cost=1000)
                continue
            owner, below = lowest(level - 1), clear(level)
            for held, first, n in ((up, 0, 2), (down, 2, 3)):
                held[level] = choose(
                    n, [(None, owner, high_half, first, 0, n), (None, below, incoming, first, 0, n)]
                )
        full_up[1], full_down[1] = on_both(1, up[1]), on_both(1, down[1])

    def start_round(r, held):
        moves = [[], []]
        for level in range(max(r, 2), depth + 1):
            if level in held:
                moves[home(level)].append((level, level - r))
        groups = []
        for i in range(max(len(side) for side in moves)):
            group = [side[i] for side in moves if i < len(side)]
            masks = [1 << (group[0][1] != 1)] * cores
            choices = []
            for level, bit in group:
                masks[home(level)] = 1 << bit
                choices.append((home(level), None, held[level], 0, 0, held[level].shape[0]))
            n = held[group[0][0]].shape[0]
            operand = held[group[0][0]] if len(group) == 1 else choose(n, choices)
            groups.append((group, across(operand, *masks)))
        return groups

    def receive(groups, held, full, gate, after=()):
        for group, incoming in groups:
            incoming, _ = lax.optimization_barrier((incoming, gate))
            for level, bit in group:
                before = held[level]
                n = before.shape[0]

                def stays(position, bit=bit):
                    return position & ((2 << bit) - 1) != 1 << bit

                held[level] = choose(
                    n, [(None, stays, before, 0, 0, n), (None, lowest(bit), incoming, 0, 0, n)]
                )
                if bit == 0:
                    full[level] = on_both(level, held[level], after)

    exchanged = []
    flying_up = flying_down = ()
    for bit in range(depth):
        other = across(z, 1 << bit)
        exchanged += [(z, other)]
        if bit == 0:
            receive_first(z)
        mark = call(mark_kernel, [(8, rank)], z, cost=4000000000)
        if bit != depth - 2:
            receive(flying_down, down, full_down, z, mark)
        if bit == depth - 1:
            lowest_levels = []
            for level in range(1, depth):
                lowest_levels += [*exchanged[level - 1], full_down[level]]
            base, weight = call(
                fold_kernel, [base.shape, leaf_t.shape], base, leaf_t,
                mid_q, mid_g, mid_y, pair_q, pair_g, pair_y, *lowest_levels, after=(z,), cost=2000000000,
            )
            receive(flying_up, up, full_up, z, (weight,))
            break
        receive(flying_up, up, full_up, z, mark)
        flying_up = start_round(bit + 2, up) if bit + 2 <= depth else ()
        if bit + 2 < depth:
            flying_down = start_round(bit + 2, down)
        (z,) = call(
            functools.partial(level_kernel, bit), [tile], z, other, full_up[bit + 1],
            cost=LV[bit],
        )

    chunks = 2 * leaves
    return last_step(
        functools.partial(last_kernel, depth - 1, chunks), rhs.shape, chunks, base, weight,
        *exchanged[depth - 1], full_up[depth],
    )


def last_step(kernel, shape, chunks, *operands):
    return pl.pallas_call(
        kernel,
        out_shape=jax.ShapeDtypeStruct(shape, F32),
        in_specs=[VMEM] * len(operands),
        out_specs=HBM,
        scratch_shapes=[pltpu.VMEM(shape, F32), pltpu.SemaphoreType.DMA((chunks,))],
        compiler_params=pltpu.CompilerParams(vmem_limit_bytes=20 * 2**20),
    )(*operands)


def solution(mesh):
    both, chip = ("leaf", "panel"), "leaf"
    in_specs = (P(both, None),) + (P(both, None, None),) * 8 + (P(chip, None, None),) * 8
    return jax.shard_map(
        local, mesh=mesh, in_specs=in_specs, out_specs=P(both, None), check_vma=False
    )
```
